32 devices in a mesh: member: 2 (over y), lat: 8 (over z, core), lon: 2 (over x), lev: 1.
Axes of the slice: x: 2, y: 2, z: 4, core: 2. Of those that a mesh axis runs over, the one named last changes fastest.
Arguments:
- adjoint: float32 [6, 32, 64, 3072], P('member', 'lev', 'lat', 'lon'), parts along dimension 0, may hold values from -6 to 6
- depth: bfloat16 [32, 64, 3072], P('lev', 'lat', 'lon'), may hold values from 0.5 to 2
- zonal_coef: float32 [64], replicated, may hold values from 0.05 to 0.5
- merid_coef: float32 [64], replicated, may hold values from 0.05 to 0.5
- coriolis: float32 [64], replicated, may hold values from -0.5 to 0.5
- layer_weight: float32 [32], P('lev'), may hold values from 0.02 to 0.2
- cutoffs: int32 [64], replicated, may hold values from 0 to 1023, as said below
- polar_flags: int32 [64], replicated, may hold values from 0 to 1, as said below
Outputs:
- adjoint_next: float32 [6, 32, 64, 3072], P('member', 'lev', 'lat', 'lon'), parts along dimension 0
The draws below stay inside these ranges and needn't reach their ends.
There are 2 independent parts, one for each index of `member`. The reference program is written for one: setup_inputs(seed, part) draws one part's arguments, and reference() takes and returns one part's arrays. A program takes and returns all parts, laid end to end along the dimension named above; an argument that names none is the same for every part. Nothing has to cross between parts.
Inputs may be any that keep to these rules, and one draw needn't show every extreme that they name: cutoffs[0] is 1023 and cutoffs[63] is 0. `polar_flags`: the flagged rows form one run that starts at row 0 and one that ends at row 63; each run has 12 to 24 rows, and one of the two has exactly 24.
All inputs are finite; a program needn't handle non-finite values.
Results may differ from the reference program's by a relative error of at most 0.0003.
Values sent between devices are 32-bit elements; how exact they have to be, the bound alone decides.
A program may use at most 128 MiB of HBM per device.

```python
import math
import jax
import jax.numpy as jnp

NLON = 3072
KMAX = 1024
LEVELS = 32
NLAT = 64
POLE_ROWS = 24


def polar_runs(key):
    folded = jax.random.fold_in(key, 11)
    first_key, second_key = jax.random.split(folded)
    shorter = jax.random.randint(first_key, (), POLE_ROWS // 2, POLE_ROWS + 1)
    north_full = jax.random.randint(second_key, (), 0, 2)
    north_count = jnp.where(north_full == 0, POLE_ROWS, shorter)
    south_count = jnp.where(north_full == 0, shorter, POLE_ROWS)
    row_index = jnp.arange(NLAT, dtype=jnp.int32)
    flag_rows = jnp.logical_or(row_index < north_count, row_index >= NLAT - south_count)
    return flag_rows.astype(jnp.int32)


def draw_polar_flags(key, part):
    return polar_runs(key)


def draw_cutoffs(key, part):
    folded = jax.random.fold_in(key, 23)
    cut_rows = jax.random.randint(folded, (NLAT,), 0, KMAX)
    cut_rows = cut_rows.at[0].set(KMAX - 1)
    cut_rows = cut_rows.at[NLAT - 1].set(0)
    return cut_rows.astype(jnp.int32)


def steps_of(own_key, dims, pieces, low, high):
    loudness = 1.0
    for position, shards_of in pieces:
        steps = jax.random.uniform(jax.random.fold_in(jax.random.fold_in(own_key, 6), position), (shards_of,), jnp.float32, low / len(pieces), high / len(pieces))
        loudness = loudness * jnp.repeat(jnp.exp(steps), dims[position] // shards_of).reshape((-1,) + (1,) * (len(dims) - 1 - position))
    return loudness


def normal_values(key, extent, spread, limit, pieces=(), kind=jnp.bfloat16):
    values = spread * jax.random.normal(key, extent, jnp.float32)
    if pieces:
        values = values * steps_of(key, extent, pieces, -0.22, 0.18)
    return jnp.clip(values, -limit, limit).astype(kind)


def setup_inputs(seed: int = 0, part: int = 0) -> dict:
    keys = jax.random.split(jax.random.key(seed), 9)
    own_keys = jax.random.split(jax.random.fold_in(keys[8], part), 9)
    adjoint = normal_values(own_keys[0], (3, LEVELS, NLAT, NLON), 1.0, 6.0, ((2, 8), (3, 2)), jnp.float32)
    depth = jnp.clip(0.5 + 1.5 * jax.random.uniform(keys[1], (LEVELS, NLAT, NLON), jnp.float32) ** steps_of(keys[1], (LEVELS, NLAT, NLON), ((1, 8), (2, 2)), -0.2, 0.2), 0.5, 2.0).astype(jnp.bfloat16)
    zonal_coef = jnp.clip(jnp.exp(jax.random.uniform(keys[2], (NLAT,), jnp.float32, math.log(0.05), math.log(0.5))), 0.05, 0.5)
    merid_coef = jnp.clip(jnp.exp(jax.random.uniform(keys[3], (NLAT,), jnp.float32, math.log(0.05), math.log(0.5))), 0.05, 0.5)
    coriolis = jnp.clip(jax.random.uniform(keys[4], (NLAT,), jnp.float32, -0.5, 0.5), -0.5, 0.5)
    layer_weight = jnp.clip(jnp.exp(jax.random.uniform(keys[5], (LEVELS,), jnp.float32, math.log(0.02), math.log(0.2))), 0.02, 0.2)
    cutoffs = draw_cutoffs(jax.random.fold_in(keys[8], 71), part)
    polar_flags = draw_polar_flags(jax.random.fold_in(keys[8], 71), part)
    return dict(adjoint=adjoint, depth=depth, zonal_coef=zonal_coef, merid_coef=merid_coef, coriolis=coriolis, layer_weight=layer_weight, cutoffs=cutoffs, polar_flags=polar_flags)


def zonal_adjoint(field, zonal_rows):
    return zonal_rows * (jnp.roll(field, 1, axis=-1) - jnp.roll(field, -1, axis=-1))


def merid_adjoint(field, merid_rows):
    scaled = merid_rows * field
    padded = jnp.pad(scaled, ((0, 0), (1, 1), (0, 0)))
    return padded[:, :-2] - padded[:, 2:]


def reference(adjoint, depth, zonal_coef, merid_coef, coriolis, layer_weight, cutoffs, polar_flags):
    spectrum = jnp.fft.rfft(adjoint, axis=-1)
    wave_index = jnp.arange(NLON // 2 + 1, dtype=jnp.int32)
    kept_modes = (wave_index[None, :] <= cutoffs[:, None]).astype(jnp.float32)
    smoothed = jnp.fft.irfft(spectrum * kept_modes[None, None, :, :], n=NLON, axis=-1).astype(jnp.float32)
    filtered = jnp.where(polar_flags[None, None, :, None] > 0, smoothed, adjoint)
    q_height = filtered[0]
    q_east = filtered[1]
    q_north = filtered[2]
    zonal_rows = zonal_coef[None, :, None]
    merid_rows = merid_coef[None, :, None]
    coriolis_rows = coriolis[None, :, None]
    height_flux = depth.astype(jnp.float32) * q_height
    column_force = -zonal_adjoint(q_east, zonal_rows) - merid_adjoint(q_north, merid_rows)
    column_sum = jnp.cumsum(column_force, axis=0)
    new_height = adjoint[0] + layer_weight[:, None, None] * column_sum
    new_east = adjoint[1] - zonal_adjoint(height_flux, zonal_rows) - coriolis_rows * q_north
    new_north = adjoint[2] - merid_adjoint(height_flux, merid_rows) + coriolis_rows * q_east
    return jnp.stack([new_height, new_east, new_north])
```

```python
import functools
import math

import jax
import jax.numpy as jnp
import ml_dtypes
import numpy as np
from jax import lax
from jax.experimental import pallas as pl
from jax.experimental.pallas import tpu as pltpu
from jax.sharding import PartitionSpec as P

KMAX = 1024
POLE_ROWS = 24


def extended(cells, sides, width, closed):
    for axis, dim in sides:
        count = lax.axis_size(axis)
        ends = count if closed else count - 1
        head = lax.slice_in_dim(cells, 0, width, axis=dim)
        tail = lax.slice_in_dim(cells, cells.shape[dim] - width, cells.shape[dim], axis=dim)
        cells = jnp.concatenate(
            [
                lax.ppermute(tail, axis, [(i, (i + 1) % count) for i in range(ends)]),
                cells,
                lax.ppermute(head, axis, [((i + 1) % count, i) for i in range(ends)]),
            ],
            axis=dim,
        )
    return cells


def entering(value, axis, join, neutral):
    count, mine = (lax.axis_size(axis), lax.axis_index(axis))
    pieces = lax.all_gather(value, axis)
    total = jnp.full_like(value, 0) + jnp.asarray(neutral, value.dtype)

    def turn(position, total):
        longer = join(total, pieces[position])
        return jnp.where(position < mine, longer, total)

    return lax.fori_loop(0, count - 1, turn, total)


def wave_table(col_count, wave_start, wave_count, circle):
    columns = lax.iota(jnp.int32, col_count)
    wave_index = wave_start + lax.iota(jnp.int32, wave_count)
    phase = columns[:, None] * wave_index[None, :] % circle
    angle = phase.astype(jnp.float32) * (2.0 * math.pi / circle)
    return jnp.concatenate([jnp.cos(angle), jnp.sin(angle)], axis=1)


def keep_weights(cut_rows, wave_start, wave_count, circle):
    wave_index = wave_start + lax.iota(jnp.int32, wave_count)
    factor = jnp.where(wave_index == 0, 1.0, 2.0) / circle
    kept = (wave_index[None, :] <= cut_rows[:, None]).astype(jnp.float32) * factor[None, :]
    return jnp.concatenate([kept, kept], axis=1)


def block_width():
    return min(KMAX, 128)


def project_rows(row_data, cut_rows):
    circle = row_data.shape[1]
    width = block_width()
    result = jnp.zeros(row_data.shape, jnp.float32)
    for block_index in range(KMAX // width):
        table = wave_table(circle, block_index * width, width, circle)
        coefs = jnp.dot(
            row_data, table, precision=lax.Precision.HIGHEST, preferred_element_type=jnp.float32
        )
        weights = keep_weights(cut_rows, block_index * width, width, circle)
        result = result + jnp.dot(
            coefs * weights,
            table.T,
            precision=lax.Precision.HIGHEST,
            preferred_element_type=jnp.float32,
        )
    return result


def transpose_filter(row_data, cut_rows, flag_rows):
    lon_count = lax.axis_size("lon")
    lon_index = lax.axis_index("lon")
    share = row_data.shape[0] // lon_count
    full_rows = lax.all_to_all(row_data, "lon", split_axis=0, concat_axis=1, tiled=True)
    my_cuts = lax.dynamic_slice_in_dim(cut_rows, lon_index * share, share)
    smoothed = project_rows(full_rows, my_cuts)
    returned = lax.all_to_all(smoothed, "lon", split_axis=1, concat_axis=0, tiled=True)
    return jnp.where(flag_rows[:, None] > 0, returned, row_data)


def polar_filter(row_data, cut_rows, flag_rows):
    return transpose_filter(row_data, cut_rows, flag_rows)


def on_device(adjoint, depth, zonal_coef, merid_coef, coriolis, layer_weight, cutoffs, polar_flags):
    fields, level_count, lat_rows, lon_cells = adjoint.shape
    lat_index = lax.axis_index("lat")
    lat_total = lat_rows * lax.axis_size("lat")
    stacked = adjoint.reshape(fields * level_count, lat_rows, lon_cells)
    bands = lax.all_to_all(stacked, "lat", split_axis=0, concat_axis=1, tiled=True)
    groups = bands.shape[0]
    polar_block = jnp.concatenate([bands[:, :POLE_ROWS], bands[:, lat_total - POLE_ROWS :]], axis=1)
    polar_cuts = jnp.concatenate([cutoffs[:POLE_ROWS], cutoffs[lat_total - POLE_ROWS :]])
    polar_marks = jnp.concatenate([polar_flags[:POLE_ROWS], polar_flags[lat_total - POLE_ROWS :]])
    row_data = polar_block.reshape(groups * 2 * POLE_ROWS, lon_cells)
    cut_rows = jnp.tile(polar_cuts, groups)
    flag_rows = jnp.tile(polar_marks, groups)
    treated = polar_filter(row_data, cut_rows, flag_rows)
    treated = treated.reshape(groups, 2 * POLE_ROWS, lon_cells)
    bands = jnp.concatenate(
        [
            treated[:, :POLE_ROWS],
            bands[:, POLE_ROWS : lat_total - POLE_ROWS],
            treated[:, POLE_ROWS:],
        ],
        axis=1,
    )
    filtered = lax.all_to_all(bands, "lat", split_axis=1, concat_axis=0, tiled=True).reshape(
        adjoint.shape
    )
    q_height = filtered[0]
    q_east = filtered[1]
    q_north = filtered[2]
    zonal_rows = lax.dynamic_slice_in_dim(zonal_coef, lat_index * lat_rows, lat_rows)[None, :, None]
    merid_rows = lax.dynamic_slice_in_dim(merid_coef, lat_index * lat_rows, lat_rows)[None, :, None]
    coriolis_rows = lax.dynamic_slice_in_dim(coriolis, lat_index * lat_rows, lat_rows)[
        None, :, None
    ]
    height_flux = depth.astype(jnp.float32) * q_height
    north_pair = jnp.stack([merid_rows * q_north, merid_rows * height_flux])
    north_rims = extended(north_pair, (("lat", 2),), 1, False)
    merid_diff = north_rims[:, :, :-2] - north_rims[:, :, 2:]
    east_pair = jnp.stack([q_east, height_flux])
    east_rims = extended(east_pair, (("lon", 3),), 1, True)
    zonal_diff = zonal_rows * (east_rims[..., :-2] - east_rims[..., 2:])
    column_force = -zonal_diff[0] - merid_diff[0]
    running = jnp.cumsum(column_force, axis=0)
    carried = entering(
        jnp.sum(column_force, axis=0), "lev", jnp.add, jnp.zeros((lat_rows, lon_cells), jnp.float32)
    )
    new_height = adjoint[0] + layer_weight[:, None, None] * (running + carried[None])
    new_east = adjoint[1] - zonal_diff[1] - coriolis_rows * q_north
    new_north = adjoint[2] - merid_diff[1] + coriolis_rows * q_east
    return jnp.stack([new_height, new_east, new_north])


RANK = 60
TILE = 256
LANES = 128


def halves(value):
    high = value.astype(jnp.bfloat16)
    return high, (value - high.astype(jnp.float32)).astype(jnp.bfloat16)


def split_table(value):
    high = np.asarray(value, np.float32).astype(ml_dtypes.bfloat16)
    low = (np.asarray(value, np.float32) - high.astype(np.float32)).astype(ml_dtypes.bfloat16)
    return high, low


@functools.lru_cache(maxsize=None)
def kernel_tables(cells):
    circle = 2 * cells

    def kernel(distance):
        wave = circle * np.sin(np.pi * (distance % (2 * circle)) / circle)
        return np.where(distance % circle == 0, 0.0, 1.0 / np.where(distance % circle == 0, 1.0, wave))

    n = np.arange(cells)
    rest = kernel(n[:, None] - n[None, :] - cells)
    columns, rows = [], []
    for _ in range(RANK):
        i, j = divmod(int(np.argmax(np.abs(rest))), cells)
        pivot = rest[i, j]
        size = np.sqrt(abs(pivot))
        u, v = rest[:, j] / pivot * size, rest[i, :] / size
        columns.append(u)
        rows.append(v)
        rest = rest - u[:, None] * v[None, :]
    project = np.stack(
        rows
        + [kernel(cells - 1 - n), kernel(0 - n), kernel(cells - 1 - n - cells), kernel(0 - n - cells)],
        axis=1,
    )
    expand = np.zeros((64, cells))
    expand[:RANK] = np.stack(columns)
    band = kernel(np.arange(2 * cells)[None, :] - np.arange(LANES)[:, None] - cells)
    return project, expand, band.astype(np.float32)


def project_kernel(x_ref, trig_ref, mix_ref, edge_ref, depth_ref, table_ref, out_ref):
    x = x_ref[...]
    fields, levels, rows, cells = x.shape
    cos, sin = trig_ref[0][None, None], trig_ref[1][None, None]

    def spectrum(value):
        high, low = halves(value.reshape(fields * levels * rows, cells))
        total = jnp.dot(high, table_ref[...], preferred_element_type=jnp.float32)
        total = total + jnp.dot(low, table_ref[...], preferred_element_type=jnp.float32)
        total = total + pltpu.roll(total, 64, 1)
        return total.reshape(fields, levels, rows, LANES)

    z = mix_ref[0][None, None] * spectrum(x * cos) + mix_ref[1][None, None] * spectrum(x * sin)
    lane = lax.broadcasted_iota(jnp.int32, (1, 1, rows, LANES), 3)
    z = z + jnp.where(lane == RANK, edge_ref[0][None, None] * x[..., cells - 1 :], 0.0)
    z = z + jnp.where(lane == RANK + 1, edge_ref[0][None, None] * x[..., :1], 0.0)
    depth = depth_ref[...].astype(jnp.float32)
    z = z + jnp.where(lane == 124, depth[None, :, :, cells - 1 :], 0.0)
    z = z + jnp.where(lane == 125, depth[None, :, :, :1], 0.0)
    out_ref[...] = z


def local_kernel(x_ref, trig_ref, inner_ref, band_ref, y_ref, high_ref, low_ref, band_high, band_low, total_ref):
    row = pl.program_id(0)
    cells = trig_ref.shape[2] // 2
    lines = cells // LANES * 8
    count = x_ref.shape[0] // lines
    blocks = cells // TILE

    def strip(block):
        return pl.ds(block * 8 + row, count, stride=lines)

    for block in range(blocks):
        x = jnp.concatenate([x_ref[strip(2 * block), :], x_ref[strip(2 * block + 1), :]], axis=1)
        high, low = halves(x)
        high_ref[pl.ds(block * count, count), :] = high
        low_ref[pl.ds(block * count, count), :] = low
    inner_cos, inner_sin = inner_ref[0, 0], inner_ref[0, 1]
    for block in range(2 * cells // LANES):
        at = pl.ds(block * LANES, LANES)
        value = band_ref[:, at] * (trig_ref[0, 1:2, at] * inner_cos - trig_ref[0, 0:1, at] * inner_sin)
        high, low = halves(value)
        band_high[:, at] = high
        band_low[:, at] = low
    for shift in [0] + [s * e for e in range(1, blocks) for s in (1, -1)]:
        first = cells + TILE * shift
        weights = [
            jnp.concatenate([band[:, first : first + TILE], band[:, first - LANES : first - LANES + TILE]], axis=0)
            for band in (band_high, band_low)
        ]
        start, stop = max(0, -shift), min(blocks, blocks - shift)
        source = pl.ds(start * count, (stop - start) * count)
        target = pl.ds((start + shift) * count, (stop - start) * count)
        value = jnp.dot(high_ref[source, :], weights[0], preferred_element_type=jnp.float32)
        value = value + jnp.dot(low_ref[source, :], weights[0], preferred_element_type=jnp.float32)
        value = value + jnp.dot(high_ref[source, :], weights[1], preferred_element_type=jnp.float32)
        if shift == 0:
            total_ref[target, :] = value
        else:
            total_ref[target, :] += value
    for block in range(blocks):
        total = total_ref[pl.ds(block * count, count), :]
        y_ref[strip(2 * block), :] = total[:, :LANES]
        y_ref[strip(2 * block + 1), :] = total[:, LANES:]


def join_kernel(x_ref, y_ref, z_ref, trig_ref, coef_ref, depth_ref, expand_ref, q_ref, first_ref, last_ref):
    fields, levels, rows, cells = x_ref.shape
    high, low = halves(z_ref[...].reshape(fields * levels * rows, LANES))

    def expanded(turn):
        part = pl.ds(turn * cells, cells)
        value = jnp.dot(high, expand_ref[0, :, part], preferred_element_type=jnp.float32)
        value = value + jnp.dot(low, expand_ref[0, :, part], preferred_element_type=jnp.float32)
        value = value + jnp.dot(high, expand_ref[1, :, part], preferred_element_type=jnp.float32)
        return value.reshape(fields, levels, rows, cells)

    coef = coef_ref[...]
    q = y_ref[...] + coef[:, 3:4][None, None] * x_ref[...]
    q = q + trig_ref[0][None, None] * expanded(0)
    q = q + trig_ref[1][None, None] * expanded(1)
    q_ref[...] = q
    merid = coef[:, 1:2][None]
    north = merid * q[2]
    flux = merid * (depth_ref[...].astype(jnp.float32) * q[0])
    for side, ref in ((0, first_ref), (rows - 1, last_ref)):
        ref[0] = north[:, side, :]
        ref[1] = flux[:, side, :]


def stencil_kernel(weight_ref, x_ref, q_ref, depth_ref, coef_ref, before_ref, after_ref, rims_ref, out_ref, run_ref):
    step = pl.program_id(0)
    _, levels, rows, cells = x_ref.shape
    coef = coef_ref[...]
    zonal, merid, coriolis = coef[:, 0:1], coef[:, 1:2], coef[:, 2:3]
    row = lax.broadcasted_iota(jnp.int32, (rows, cells), 0)
    column = lax.broadcasted_iota(jnp.int32, (rows, cells), 1)

    def zonal_adjoint(value, west, east):
        left = jnp.where(column == 0, west, pltpu.roll(value, 1, 1))
        right = jnp.where(column == cells - 1, east, pltpu.roll(value, cells - 1, 1))
        return zonal * (left - right)

    def merid_adjoint(value, before, after):
        value = merid * value
        up = jnp.where(row == 0, before, pltpu.roll(value, 1, 0))
        down = jnp.where(row == rows - 1, after, pltpu.roll(value, rows - 1, 0))
        return up - down

    @pl.when(step == 0)
    def _():
        run_ref[...] = jnp.zeros_like(run_ref)

    for level in range(levels):
        height, east, north = q_ref[0, level], q_ref[1, level], q_ref[2, level]
        flux = depth_ref[level].astype(jnp.float32) * height
        rims = rims_ref[level]
        line = pl.ds(level, 1)
        run_ref[...] -= zonal_adjoint(east, rims[:, 0:1], rims[:, 1:2]) + merid_adjoint(
            north, before_ref[0, line, :], after_ref[0, line, :]
        )
        out_ref[0, level] = x_ref[0, level] + weight_ref[step * levels + level] * run_ref[...]
        out_ref[1, level] = x_ref[1, level] - zonal_adjoint(flux, rims[:, 2:3], rims[:, 3:4]) - coriolis * north
        out_ref[2, level] = (
            x_ref[2, level]
            - merid_adjoint(flux, before_ref[1, line, :], after_ref[1, line, :])
            + coriolis * east
        )


def whole(array):
    shape = array.shape
    return pl.BlockSpec(shape, lambda *_: (0,) * len(shape))


def on_pair(adjoint, depth, zonal_coef, merid_coef, coriolis, layer_weight, cutoffs, polar_flags):
    fields, level_count, rows, cells = adjoint.shape
    circle = 2 * cells
    lat_count = lax.axis_size("lat")
    first_row = lax.axis_index("lat") * rows
    project, expand, band = kernel_tables(cells)
    project_high, project_low = split_table(project)
    project_table = jnp.asarray(np.concatenate([project_high, project_low], axis=1))
    nothing = np.zeros_like(expand)
    expand_table = jnp.asarray(
        np.stack(split_table(np.block([[expand, nothing], [nothing, expand]])))
    )

    def mine(values):
        return lax.dynamic_slice_in_dim(values, first_row, rows)

    cuts, flags = mine(cutoffs), mine(polar_flags)
    kept = 2 * cuts + 1
    offsets = lax.iota(jnp.int32, circle) - cells
    phase = (kept[:, None] * offsets[None, :]) % (2 * circle)
    angle = phase.astype(jnp.float32) * (math.pi / circle)
    cos, sin = jnp.cos(angle), jnp.sin(angle)
    on = (flags > 0).astype(jnp.float32)[:, None]
    keep = jnp.where(flags > 0, kept.astype(jnp.float32) / circle, 1.0)[:, None]
    sign = on * jnp.where(cuts % 2 == 0, -1.0, 1.0)[:, None]
    own_cos, own_sin = cos[:, cells:], sin[:, cells:]
    trig = jnp.stack([own_cos, own_sin])
    cross = jnp.stack([sign * own_cos, sign * own_sin])
    outer = jnp.stack([on * cos, on * sin], axis=1)
    inner = jnp.stack([own_cos[:, :LANES], own_sin[:, :LANES]], axis=1)[..., None]
    one, zero = jnp.ones((rows, RANK), jnp.float32), jnp.zeros((rows, RANK), jnp.float32)
    blank = jnp.zeros((rows, 4), jnp.float32)
    end_cos, end_sin = own_cos[:, cells - 1 :], own_sin[:, cells - 1 :]
    start_cos, start_sin = own_cos[:, :1], own_sin[:, :1]
    mix = jnp.stack(
        [
            jnp.concatenate(
                [one, on * end_sin, on * start_sin, sign * end_cos, sign * start_cos, zero, blank], axis=1
            ),
            jnp.concatenate(
                [zero, -on * end_cos, -on * start_cos, sign * end_sin, sign * start_sin, one, blank], axis=1
            ),
        ]
    )
    coef = jnp.concatenate(
        [
            mine(zonal_coef)[:, None],
            mine(merid_coef)[:, None],
            mine(coriolis)[:, None],
            keep,
            jnp.zeros((rows, LANES - 4), jnp.float32),
        ],
        axis=1,
    )
    edge = keep[None]

    part = 8
    steps = level_count // part
    four = pl.BlockSpec((fields, part, rows, cells), lambda i: (0, i, 0, 0))
    three = pl.BlockSpec((part, rows, cells), lambda i: (i, 0, 0))
    code = pl.BlockSpec((fields, part, rows, LANES), lambda i: (0, i, 0, 0))
    lines = pl.BlockSpec((2, part, cells), lambda i: (0, i, 0))
    limit = pltpu.CompilerParams(vmem_limit_bytes=48 * 2**20)
    count = fields * level_count * rows

    z = pl.pallas_call(
        project_kernel,
        grid=(steps,),
        in_specs=[four, whole(trig), whole(mix), whole(edge), three, whole(project_table)],
        out_specs=code,
        out_shape=jax.ShapeDtypeStruct((fields, level_count, rows, LANES), jnp.float32),
        compiler_params=limit,
    )(adjoint, trig, mix, edge, depth, project_table)
    arrived = lax.ppermute(z, "lon", [(0, 1), (1, 0)])

    tiles = (fields * level_count, rows, cells // LANES, LANES)
    flat = adjoint.reshape(tiles).transpose(0, 2, 1, 3).reshape(-1, LANES)
    strip = count // rows * cells // TILE
    y = pl.pallas_call(
        local_kernel,
        grid=(rows,),
        in_specs=[
            whole(flat),
            pl.BlockSpec((1, 2, circle), lambda i: (i, 0, 0)),
            pl.BlockSpec((1, 2, LANES, 1), lambda i: (i, 0, 0, 0)),
            whole(band),
        ],
        out_specs=whole(flat),
        out_shape=jax.ShapeDtypeStruct(flat.shape, jnp.float32),
        scratch_shapes=[
            pltpu.VMEM((strip, TILE), jnp.bfloat16),
            pltpu.VMEM((strip, TILE), jnp.bfloat16),
            pltpu.VMEM((LANES, circle), jnp.bfloat16),
            pltpu.VMEM((LANES, circle), jnp.bfloat16),
            pltpu.VMEM((strip, TILE), jnp.float32),
        ],
        cost_estimate=pl.CostEstimate(
            flops=6 * count * cells * cells, bytes_accessed=8 * count * cells, transcendentals=0
        ),
        compiler_params=limit,
    )(flat, outer, inner, jnp.asarray(band))

    y = y.reshape(tiles[0], tiles[2], rows, LANES).transpose(0, 2, 1, 3).reshape(adjoint.shape)
    edges = jax.ShapeDtypeStruct((2, level_count, cells), jnp.float32)
    q, first, last = pl.pallas_call(
        join_kernel,
        grid=(steps,),
        in_specs=[four, four, code, whole(cross), whole(coef), three, whole(expand_table)],
        out_specs=[four, lines, lines],
        out_shape=[jax.ShapeDtypeStruct(adjoint.shape, jnp.float32), edges, edges],
        compiler_params=limit,
    )(adjoint, y, arrived, cross, coef, depth, expand_table)
    before = lax.ppermute(last, "lat", [(i, i + 1) for i in range(lat_count - 1)])
    after = lax.ppermute(first, "lat", [(i + 1, i) for i in range(lat_count - 1)])

    rims = arrived[:2, ..., RANK : RANK + 2] + z[:2, ..., RANK + 2 : RANK + 4]
    rims = jnp.concatenate([rims[1], rims[0] * arrived[0, ..., 124:126]], axis=-1)
    return pl.pallas_call(
        stencil_kernel,
        grid=(steps,),
        in_specs=[
            pl.BlockSpec(memory_space=pltpu.SMEM),
            four,
            four,
            three,
            whole(coef),
            lines,
            lines,
            pl.BlockSpec((part, rows, 4), lambda i: (i, 0, 0)),
        ],
        out_specs=four,
        out_shape=jax.ShapeDtypeStruct(adjoint.shape, jnp.float32),
        scratch_shapes=[pltpu.VMEM((rows, cells), jnp.float32)],
        compiler_params=limit,
    )(layer_weight, adjoint, q, depth, coef, before, after, rims)


def plan_for(mesh):
    return on_pair if mesh.shape["lon"] == 2 and mesh.shape["lev"] == 1 else on_device


def solution(mesh):
    return jax.shard_map(
        plan_for(mesh),
        mesh=mesh,
        in_specs=(
            P("member", "lev", "lat", "lon"),
            P("lev", "lat", "lon"),
            P(),
            P(),
            P(),
            P("lev"),
            P(),
            P(),
        ),
        out_specs=P("member", "lev", "lat", "lon"),
        check_vma=False,
    )
```

```python
import functools
import math

import jax
import jax.numpy as jnp
import ml_dtypes
import numpy as np
from jax import lax
from jax.experimental import pallas as pl
from jax.experimental.pallas import tpu as pltpu
from jax.sharding import PartitionSpec as P

KMAX = 1024
POLE_ROWS = 24


def extended(cells, sides, width, closed):
    for axis, dim in sides:
        count = lax.axis_size(axis)
        ends = count if closed else count - 1
        head = lax.slice_in_dim(cells, 0, width, axis=dim)
        tail = lax.slice_in_dim(cells, cells.shape[dim] - width, cells.shape[dim], axis=dim)
        cells = jnp.concatenate(
            [
                lax.ppermute(tail, axis, [(i, (i + 1) % count) for i in range(ends)]),
                cells,
                lax.ppermute(head, axis, [((i + 1) % count, i) for i in range(ends)]),
            ],
            axis=dim,
        )
    return cells


def entering(value, axis, join, neutral):
    count, mine = (lax.axis_size(axis), lax.axis_index(axis))
    pieces = lax.all_gather(value, axis)
    total = jnp.full_like(value, 0) + jnp.asarray(neutral, value.dtype)

    def turn(position, total):
        longer = join(total, pieces[position])
        return jnp.where(position < mine, longer, total)

    return lax.fori_loop(0, count - 1, turn, total)


def wave_table(col_count, wave_start, wave_count, circle):
    columns = lax.iota(jnp.int32, col_count)
    wave_index = wave_start + lax.iota(jnp.int32, wave_count)
    phase = columns[:, None] * wave_index[None, :] % circle
    angle = phase.astype(jnp.float32) * (2.0 * math.pi / circle)
    return jnp.concatenate([jnp.cos(angle), jnp.sin(angle)], axis=1)


def keep_weights(cut_rows, wave_start, wave_count, circle):
    wave_index = wave_start + lax.iota(jnp.int32, wave_count)
    factor = jnp.where(wave_index == 0, 1.0, 2.0) / circle
    kept = (wave_index[None, :] <= cut_rows[:, None]).astype(jnp.float32) * factor[None, :]
    return jnp.concatenate([kept, kept], axis=1)


def block_width():
    return min(KMAX, 128)


def project_rows(row_data, cut_rows):
    circle = row_data.shape[1]
    width = block_width()
    result = jnp.zeros(row_data.shape, jnp.float32)
    for block_index in range(KMAX // width):
        table = wave_table(circle, block_index * width, width, circle)
        coefs = jnp.dot(
            row_data, table, precision=lax.Precision.HIGHEST, preferred_element_type=jnp.float32
        )
        weights = keep_weights(cut_rows, block_index * width, width, circle)
        result = result + jnp.dot(
            coefs * weights,
            table.T,
            precision=lax.Precision.HIGHEST,
            preferred_element_type=jnp.float32,
        )
    return result


def transpose_filter(row_data, cut_rows, flag_rows):
    lon_count = lax.axis_size("lon")
    lon_index = lax.axis_index("lon")
    share = row_data.shape[0] // lon_count
    full_rows = lax.all_to_all(row_data, "lon", split_axis=0, concat_axis=1, tiled=True)
    my_cuts = lax.dynamic_slice_in_dim(cut_rows, lon_index * share, share)
    smoothed = project_rows(full_rows, my_cuts)
    returned = lax.all_to_all(smoothed, "lon", split_axis=1, concat_axis=0, tiled=True)
    return jnp.where(flag_rows[:, None] > 0, returned, row_data)


def polar_filter(row_data, cut_rows, flag_rows):
    return transpose_filter(row_data, cut_rows, flag_rows)


def on_device(adjoint, depth, zonal_coef, merid_coef, coriolis, layer_weight, cutoffs, polar_flags):
    fields, level_count, lat_rows, lon_cells = adjoint.shape
    lat_index = lax.axis_index("lat")
    lat_total = lat_rows * lax.axis_size("lat")
    stacked = adjoint.reshape(fields * level_count, lat_rows, lon_cells)
    bands = lax.all_to_all(stacked, "lat", split_axis=0, concat_axis=1, tiled=True)
    groups = bands.shape[0]
    polar_block = jnp.concatenate([bands[:, :POLE_ROWS], bands[:, lat_total - POLE_ROWS :]], axis=1)
    polar_cuts = jnp.concatenate([cutoffs[:POLE_ROWS], cutoffs[lat_total - POLE_ROWS :]])
    polar_marks = jnp.concatenate([polar_flags[:POLE_ROWS], polar_flags[lat_total - POLE_ROWS :]])
    row_data = polar_block.reshape(groups * 2 * POLE_ROWS, lon_cells)
    cut_rows = jnp.tile(polar_cuts, groups)
    flag_rows = jnp.tile(polar_marks, groups)
    treated = polar_filter(row_data, cut_rows, flag_rows)
    treated = treated.reshape(groups, 2 * POLE_ROWS, lon_cells)
    bands = jnp.concatenate(
        [
            treated[:, :POLE_ROWS],
            bands[:, POLE_ROWS : lat_total - POLE_ROWS],
            treated[:, POLE_ROWS:],
        ],
        axis=1,
    )
    filtered = lax.all_to_all(bands, "lat", split_axis=1, concat_axis=0, tiled=True).reshape(
        adjoint.shape
    )
    q_height = filtered[0]
    q_east = filtered[1]
    q_north = filtered[2]
    zonal_rows = lax.dynamic_slice_in_dim(zonal_coef, lat_index * lat_rows, lat_rows)[None, :, None]
    merid_rows = lax.dynamic_slice_in_dim(merid_coef, lat_index * lat_rows, lat_rows)[None, :, None]
    coriolis_rows = lax.dynamic_slice_in_dim(coriolis, lat_index * lat_rows, lat_rows)[
        None, :, None
    ]
    height_flux = depth.astype(jnp.float32) * q_height
    north_pair = jnp.stack([merid_rows * q_north, merid_rows * height_flux])
    north_rims = extended(north_pair, (("lat", 2),), 1, False)
    merid_diff = north_rims[:, :, :-2] - north_rims[:, :, 2:]
    east_pair = jnp.stack([q_east, height_flux])
    east_rims = extended(east_pair, (("lon", 3),), 1, True)
    zonal_diff = zonal_rows * (east_rims[..., :-2] - east_rims[..., 2:])
    column_force = -zonal_diff[0] - merid_diff[0]
    running = jnp.cumsum(column_force, axis=0)
    carried = entering(
        jnp.sum(column_force, axis=0), "lev", jnp.add, jnp.zeros((lat_rows, lon_cells), jnp.float32)
    )
    new_height = adjoint[0] + layer_weight[:, None, None] * (running + carried[None])
    new_east = adjoint[1] - zonal_diff[1] - coriolis_rows * q_north
    new_north = adjoint[2] - merid_diff[1] + coriolis_rows * q_east
    return jnp.stack([new_height, new_east, new_north])


RANK = 60
TILE = 256
LANES = 128


def halves(value):
    high = value.astype(jnp.bfloat16)
    return high, (value - high.astype(jnp.float32)).astype(jnp.bfloat16)


def split_table(value):
    high = np.asarray(value, np.float32).astype(ml_dtypes.bfloat16)
    low = (np.asarray(value, np.float32) - high.astype(np.float32)).astype(ml_dtypes.bfloat16)
    return high, low


@functools.lru_cache(maxsize=None)
def kernel_tables(cells):
    circle = 2 * cells

    def kernel(distance):
        wave = circle * np.sin(np.pi * (distance % (2 * circle)) / circle)
        return np.where(distance % circle == 0, 0.0, 1.0 / np.where(distance % circle == 0, 1.0, wave))

    n = np.arange(cells)
    rest = kernel(n[:, None] - n[None, :] - cells)
    columns, rows = [], []
    for _ in range(RANK):
        i, j = divmod(int(np.argmax(np.abs(rest))), cells)
        pivot = rest[i, j]
        size = np.sqrt(abs(pivot))
        u, v = rest[:, j] / pivot * size, rest[i, :] / size
        columns.append(u)
        rows.append(v)
        rest = rest - u[:, None] * v[None, :]
    project = np.stack(
        rows
        + [kernel(cells - 1 - n), kernel(0 - n), kernel(cells - 1 - n - cells), kernel(0 - n - cells)],
        axis=1,
    )
    expand = np.zeros((64, cells))
    expand[:RANK] = np.stack(columns)
    band = kernel(np.arange(2 * cells)[None, :] - np.arange(LANES)[:, None] - cells)
    return project, expand, band.astype(np.float32)


def project_kernel(x_ref, trig_ref, mix_ref, edge_ref, depth_ref, table_ref, out_ref):
    x = x_ref[...]
    fields, levels, rows, cells = x.shape
    cos, sin = trig_ref[0][None, None], trig_ref[1][None, None]

    def spectrum(value):
        high, low = halves(value.reshape(fields * levels * rows, cells))
        total = jnp.dot(high, table_ref[...], preferred_element_type=jnp.float32)
        total = total + jnp.dot(low, table_ref[...], preferred_element_type=jnp.float32)
        total = total + pltpu.roll(total, 64, 1)
        return total.reshape(fields, levels, rows, LANES)

    z = mix_ref[0][None, None] * spectrum(x * cos) + mix_ref[1][None, None] * spectrum(x * sin)
    lane = lax.broadcasted_iota(jnp.int32, (1, 1, rows, LANES), 3)
    z = z + jnp.where(lane == RANK, edge_ref[0][None, None] * x[..., cells - 1 :], 0.0)
    z = z + jnp.where(lane == RANK + 1, edge_ref[0][None, None] * x[..., :1], 0.0)
    depth = depth_ref[...].astype(jnp.float32)
    z = z + jnp.where(lane == 124, depth[None, :, :, cells - 1 :], 0.0)
    z = z + jnp.where(lane == 125, depth[None, :, :, :1], 0.0)
    out_ref[...] = z


def local_row(row, x_ref, trig_ref, coef_ref, band_ref, high_ref, low_ref, band_high, band_low, total_ref):
    cells = trig_ref.shape[2] // 2
    lines = cells // LANES * 8
    count = x_ref.shape[0] // lines
    blocks = cells // TILE
    chosen = lax.broadcasted_iota(jnp.int32, (8, LANES), 0) == row

    def line(values):
        return jnp.sum(jnp.where(chosen, values, 0.0), axis=0, keepdims=True)

    def strip(block):
        return pl.ds(block * 8 + row, count, stride=lines)

    coef = line(coef_ref[...])
    keep = coef[:, 3:4]
    for block in range(blocks):
        x = jnp.concatenate([x_ref[strip(2 * block), :], x_ref[strip(2 * block + 1), :]], axis=1)
        high, low = halves(x)
        at = pl.ds(block * count, count)
        high_ref[at, :] = high
        low_ref[at, :] = low
        total_ref[at, :] = keep * x

    def upright(which):
        values = coef[:, 4:5] * line(trig_ref[which, :, cells : cells + LANES])
        return jnp.broadcast_to(values, (LANES, LANES)).T

    inner_cos, inner_sin = upright(0), upright(1)
    for block in range(2 * cells // LANES):
        at = pl.ds(block * LANES, LANES)
        value = band_ref[:, at] * (line(trig_ref[1, :, at]) * inner_cos - line(trig_ref[0, :, at]) * inner_sin)
        high, low = halves(value)
        band_high[:, at] = high
        band_low[:, at] = low
    for shift in range(1 - blocks, blocks):
        first = cells + TILE * shift
        weights = [
            jnp.concatenate([band[:, first : first + TILE], band[:, first - LANES : first - LANES + TILE]], axis=0)
            for band in (band_high, band_low)
        ]
        start, stop = max(0, -shift), min(blocks, blocks - shift)
        source = pl.ds(start * count, (stop - start) * count)
        target = pl.ds((start + shift) * count, (stop - start) * count)
        value = jnp.dot(high_ref[source, :], weights[0], preferred_element_type=jnp.float32)
        value = value + jnp.dot(low_ref[source, :], weights[0], preferred_element_type=jnp.float32)
        value = value + jnp.dot(high_ref[source, :], weights[1], preferred_element_type=jnp.float32)
        total_ref[target, :] += value


def rim_kernel(x_ref, trig_ref, coef_ref, band_ref, y_ref, *scratch):
    local_row(pl.program_id(0) * 7, x_ref, trig_ref, coef_ref, band_ref, *scratch)
    total_ref = scratch[-1]
    count = y_ref.shape[1]
    for block in range(y_ref.shape[2] // TILE):
        y_ref[0, :, pl.ds(block * TILE, TILE)] = total_ref[pl.ds(block * count, count), :]


def inner_kernel(x_ref, trig_ref, coef_ref, band_ref, rim_ref, sent_ref, y_ref, *scratch):
    del sent_ref
    row = pl.program_id(0)
    _, count, cells = rim_ref.shape
    lines = cells // LANES * 8
    total_ref = scratch[-1]
    is_rim = jnp.logical_or(row == 0, row == 7)

    @pl.when(jnp.logical_not(is_rim))
    def _():
        local_row(row, x_ref, trig_ref, coef_ref, band_ref, *scratch)
        for block in range(cells // LANES):
            value = total_ref[pl.ds(block // 2 * count, count), pl.ds(block % 2 * LANES, LANES)]
            y_ref[pl.ds(block * 8 + row, count, stride=lines), :] = value

    @pl.when(is_rim)
    def _():
        for block in range(cells // LANES):
            value = rim_ref[row // 7, :, pl.ds(block * LANES, LANES)]
            y_ref[pl.ds(block * 8 + row, count, stride=lines), :] = value


def expanded(z, expand_ref, part):
    high, low = halves(z)
    value = jnp.dot(high, expand_ref[0, :, part], preferred_element_type=jnp.float32)
    value = value + jnp.dot(low, expand_ref[0, :, part], preferred_element_type=jnp.float32)
    return value + jnp.dot(high, expand_ref[1, :, part], preferred_element_type=jnp.float32)


def border_kernel(z_ref, y_ref, trig_ref, coef_ref, depth_ref, expand_ref, first_ref, last_ref):
    _, count, cells = y_ref.shape
    levels = depth_ref.shape[0]
    depth = depth_ref[...].astype(jnp.float32)
    for turn, row, ref in ((0, 0, first_ref), (1, 7, last_ref)):
        z = z_ref[pl.ds(row, count, stride=8), :]
        q = y_ref[turn]
        q = q + trig_ref[0, row : row + 1] * expanded(z, expand_ref, pl.ds(0, cells))
        q = q + trig_ref[1, row : row + 1] * expanded(z, expand_ref, pl.ds(cells, cells))
        merid = coef_ref[row : row + 1, 1:2]
        ref[0] = merid * q[2 * levels :]
        ref[1] = merid * (depth[:, row, :] * q[:levels])


def final_kernel(
    weight_ref, x_ref, y_ref, z_ref, trig_ref, coef_ref, depth_ref, expand_ref, before_ref, after_ref, rims_ref,
    out_ref, q_ref, run_ref,
):
    step = pl.program_id(0)
    fields, levels, rows, cells = x_ref.shape
    coef = coef_ref[...]
    zonal, merid, coriolis = coef[:, 0:1], coef[:, 1:2], coef[:, 2:3]
    row = lax.broadcasted_iota(jnp.int32, (rows, cells), 0)
    column = lax.broadcasted_iota(jnp.int32, (rows, cells), 1)

    z = z_ref[...].reshape(fields * levels * rows, LANES)
    q = y_ref[...]
    for turn in range(2):
        value = expanded(z, expand_ref, pl.ds(turn * cells, cells))
        q = q + trig_ref[turn][None, None] * value.reshape(fields, levels, rows, cells)
    q_ref[...] = q

    def zonal_adjoint(value, west, east):
        left = jnp.where(column == 0, west, pltpu.roll(value, 1, 1))
        right = jnp.where(column == cells - 1, east, pltpu.roll(value, cells - 1, 1))
        return zonal * (left - right)

    def merid_adjoint(value, before, after):
        value = merid * value
        up = jnp.where(row == 0, before, pltpu.roll(value, 1, 0))
        down = jnp.where(row == rows - 1, after, pltpu.roll(value, rows - 1, 0))
        return up - down

    @pl.when(step == 0)
    def _():
        run_ref[...] = jnp.zeros_like(run_ref)

    for level in range(levels):
        height, east, north = q_ref[0, level], q_ref[1, level], q_ref[2, level]
        flux = depth_ref[level].astype(jnp.float32) * height
        rims = rims_ref[level]
        line = pl.ds(level, 1)
        run_ref[...] -= zonal_adjoint(east, rims[:, 0:1], rims[:, 1:2]) + merid_adjoint(
            north, before_ref[0, line, :], after_ref[0, line, :]
        )
        out_ref[0, level] = x_ref[0, level] + weight_ref[step * levels + level] * run_ref[...]
        out_ref[1, level] = x_ref[1, level] - zonal_adjoint(flux, rims[:, 2:3], rims[:, 3:4]) - coriolis * north
        out_ref[2, level] = (
            x_ref[2, level]
            - merid_adjoint(flux, before_ref[1, line, :], after_ref[1, line, :])
            + coriolis * east
        )


def whole(array):
    shape = array.shape
    return pl.BlockSpec(shape, lambda *_: (0,) * len(shape))


def on_pair(adjoint, depth, zonal_coef, merid_coef, coriolis, layer_weight, cutoffs, polar_flags):
    fields, level_count, rows, cells = adjoint.shape
    circle = 2 * cells
    lat_count = lax.axis_size("lat")
    first_row = lax.axis_index("lat") * rows
    project, expand, band = kernel_tables(cells)
    project_high, project_low = split_table(project)
    project_table = jnp.asarray(np.concatenate([project_high, project_low], axis=1))
    nothing = np.zeros_like(expand)
    expand_table = jnp.asarray(
        np.stack(split_table(np.block([[expand, nothing], [nothing, expand]])))
    )

    def mine(values):
        return lax.dynamic_slice_in_dim(values, first_row, rows)

    cuts, flags = mine(cutoffs), mine(polar_flags)
    kept = 2 * cuts + 1
    offsets = lax.iota(jnp.int32, circle) - cells
    phase = (kept[:, None] * offsets[None, :]) % (2 * circle)
    angle = phase.astype(jnp.float32) * (math.pi / circle)
    cos, sin = jnp.cos(angle), jnp.sin(angle)
    on = (flags > 0).astype(jnp.float32)[:, None]
    keep = jnp.where(flags > 0, kept.astype(jnp.float32) / circle, 1.0)[:, None]
    sign = on * jnp.where(cuts % 2 == 0, -1.0, 1.0)[:, None]
    own_cos, own_sin = cos[:, cells:], sin[:, cells:]
    trig = jnp.stack([own_cos, own_sin])
    cross = jnp.stack([sign * own_cos, sign * own_sin])
    around = jnp.stack([cos, sin])
    one, zero = jnp.ones((rows, RANK), jnp.float32), jnp.zeros((rows, RANK), jnp.float32)
    blank = jnp.zeros((rows, 4), jnp.float32)
    end_cos, end_sin = own_cos[:, cells - 1 :], own_sin[:, cells - 1 :]
    start_cos, start_sin = own_cos[:, :1], own_sin[:, :1]
    mix = jnp.stack(
        [
            jnp.concatenate(
                [one, on * end_sin, on * start_sin, sign * end_cos, sign * start_cos, zero, blank], axis=1
            ),
            jnp.concatenate(
                [zero, -on * end_cos, -on * start_cos, sign * end_sin, sign * start_sin, one, blank], axis=1
            ),
        ]
    )
    coef = jnp.concatenate(
        [
            mine(zonal_coef)[:, None],
            mine(merid_coef)[:, None],
            mine(coriolis)[:, None],
            keep,
            on,
            jnp.zeros((rows, LANES - 5), jnp.float32),
        ],
        axis=1,
    )
    edge = keep[None]

    part = 8
    steps = level_count // part
    four = pl.BlockSpec((fields, part, rows, cells), lambda i: (0, i, 0, 0))
    three = pl.BlockSpec((part, rows, cells), lambda i: (i, 0, 0))
    code = pl.BlockSpec((fields, part, rows, LANES), lambda i: (0, i, 0, 0))
    lines = pl.BlockSpec((2, part, cells), lambda i: (0, i, 0))
    limit = pltpu.CompilerParams(vmem_limit_bytes=48 * 2**20)
    count = fields * level_count * rows

    z = pl.pallas_call(
        project_kernel,
        grid=(steps,),
        in_specs=[four, whole(trig), whole(mix), whole(edge), three, whole(project_table)],
        out_specs=code,
        out_shape=jax.ShapeDtypeStruct((fields, level_count, rows, LANES), jnp.float32),
        compiler_params=limit,
    )(adjoint, trig, mix, edge, depth, project_table)
    arrived = lax.ppermute(z, "lon", [(0, 1), (1, 0)])

    circles = fields * level_count
    tiles = (circles, rows, cells // LANES, LANES)
    flat = adjoint.reshape(tiles).transpose(0, 2, 1, 3).reshape(-1, LANES)
    strip = circles * cells // TILE
    scratch = [
        pltpu.VMEM((strip, TILE), jnp.bfloat16),
        pltpu.VMEM((strip, TILE), jnp.bfloat16),
        pltpu.VMEM((LANES, circle), jnp.bfloat16),
        pltpu.VMEM((LANES, circle), jnp.bfloat16),
        pltpu.VMEM((strip, TILE), jnp.float32),
    ]
    band = jnp.asarray(band)

    def cost(done):
        return pl.CostEstimate(
            flops=6 * done * circles * cells * cells, bytes_accessed=8 * count * cells, transcendentals=0
        )

    rim = pl.pallas_call(
        rim_kernel,
        grid=(2,),
        in_specs=[whole(flat), whole(around), whole(coef), whole(band)],
        out_specs=pl.BlockSpec((1, circles, cells), lambda i: (i, 0, 0)),
        out_shape=jax.ShapeDtypeStruct((2, circles, cells), jnp.float32),
        scratch_shapes=scratch,
        cost_estimate=cost(2),
        compiler_params=limit,
    )(flat, around, coef, band)

    sent = arrived.reshape(count, LANES)
    edges = jax.ShapeDtypeStruct((2, level_count, cells), jnp.float32)
    first, last = pl.pallas_call(
        border_kernel,
        grid=(1,),
        in_specs=[whole(sent), whole(rim), whole(cross), whole(coef), whole(depth), whole(expand_table)],
        out_specs=[whole(edges), whole(edges)],
        out_shape=[edges, edges],
        compiler_params=limit,
    )(sent, rim, cross, coef, depth, expand_table)
    before = lax.ppermute(last, "lat", [(i, i + 1) for i in range(lat_count - 1)])
    after = lax.ppermute(first, "lat", [(i + 1, i) for i in range(lat_count - 1)])

    y = pl.pallas_call(
        inner_kernel,
        grid=(rows,),
        in_specs=[
            whole(flat),
            whole(around),
            whole(coef),
            whole(band),
            whole(rim),
            pl.BlockSpec(memory_space=pl.ANY),
        ],
        out_specs=whole(flat),
        out_shape=jax.ShapeDtypeStruct(flat.shape, jnp.float32),
        scratch_shapes=scratch,
        cost_estimate=cost(rows - 2),
        compiler_params=limit,
    )(flat, around, coef, band, rim, first)
    y = y.reshape(tiles[0], tiles[2], rows, LANES).transpose(0, 2, 1, 3).reshape(adjoint.shape)

    rims = arrived[:2, ..., RANK : RANK + 2] + z[:2, ..., RANK + 2 : RANK + 4]
    rims = jnp.concatenate([rims[1], rims[0] * arrived[0, ..., 124:126]], axis=-1)
    return pl.pallas_call(
        final_kernel,
        grid=(steps,),
        in_specs=[
            pl.BlockSpec(memory_space=pltpu.SMEM),
            four,
            four,
            code,
            whole(cross),
            whole(coef),
            three,
            whole(expand_table),
            lines,
            lines,
            pl.BlockSpec((part, rows, 4), lambda i: (i, 0, 0)),
        ],
        out_specs=four,
        out_shape=jax.ShapeDtypeStruct(adjoint.shape, jnp.float32),
        scratch_shapes=[
            pltpu.VMEM((fields, part, rows, cells), jnp.float32),
            pltpu.VMEM((rows, cells), jnp.float32),
        ],
        compiler_params=limit,
    )(layer_weight, adjoint, y, arrived, cross, coef, depth, expand_table, before, after, rims)


def plan_for(mesh):
    return on_pair if mesh.shape["lon"] == 2 and mesh.shape["lev"] == 1 else on_device


def solution(mesh):
    return jax.shard_map(
        plan_for(mesh),
        mesh=mesh,
        in_specs=(
            P("member", "lev", "lat", "lon"),
            P("lev", "lat", "lon"),
            P(),
            P(),
            P(),
            P("lev"),
            P(),
            P(),
        ),
        out_specs=P("member", "lev", "lat", "lon"),
        check_vma=False,
    )
```

```python
import functools
import math

import jax
import jax.numpy as jnp
import ml_dtypes
import numpy as np
from jax import lax
from jax.experimental import pallas as pl
from jax.experimental.pallas import tpu as pltpu
from jax.sharding import PartitionSpec as P

KMAX = 1024
POLE_ROWS = 24


def extended(cells, sides, width, closed):
    for axis, dim in sides:
        count = lax.axis_size(axis)
        ends = count if closed else count - 1
        head = lax.slice_in_dim(cells, 0, width, axis=dim)
        tail = lax.slice_in_dim(cells, cells.shape[dim] - width, cells.shape[dim], axis=dim)
        cells = jnp.concatenate(
            [
                lax.ppermute(tail, axis, [(i, (i + 1) % count) for i in range(ends)]),
                cells,
                lax.ppermute(head, axis, [((i + 1) % count, i) for i in range(ends)]),
            ],
            axis=dim,
        )
    return cells


def entering(value, axis, join, neutral):
    count, mine = (lax.axis_size(axis), lax.axis_index(axis))
    pieces = lax.all_gather(value, axis)
    total = jnp.full_like(value, 0) + jnp.asarray(neutral, value.dtype)

    def turn(position, total):
        longer = join(total, pieces[position])
        return jnp.where(position < mine, longer, total)

    return lax.fori_loop(0, count - 1, turn, total)


def wave_table(col_count, wave_start, wave_count, circle):
    columns = lax.iota(jnp.int32, col_count)
    wave_index = wave_start + lax.iota(jnp.int32, wave_count)
    phase = columns[:, None] * wave_index[None, :] % circle
    angle = phase.astype(jnp.float32) * (2.0 * math.pi / circle)
    return jnp.concatenate([jnp.cos(angle), jnp.sin(angle)], axis=1)


def keep_weights(cut_rows, wave_start, wave_count, circle):
    wave_index = wave_start + lax.iota(jnp.int32, wave_count)
    factor = jnp.where(wave_index == 0, 1.0, 2.0) / circle
    kept = (wave_index[None, :] <= cut_rows[:, None]).astype(jnp.float32) * factor[None, :]
    return jnp.concatenate([kept, kept], axis=1)


def block_width():
    return min(KMAX, 128)


def project_rows(row_data, cut_rows):
    circle = row_data.shape[1]
    width = block_width()
    result = jnp.zeros(row_data.shape, jnp.float32)
    for block_index in range(KMAX // width):
        table = wave_table(circle, block_index * width, width, circle)
        coefs = jnp.dot(
            row_data, table, precision=lax.Precision.HIGHEST, preferred_element_type=jnp.float32
        )
        weights = keep_weights(cut_rows, block_index * width, width, circle)
        result = result + jnp.dot(
            coefs * weights,
            table.T,
            precision=lax.Precision.HIGHEST,
            preferred_element_type=jnp.float32,
        )
    return result


def transpose_filter(row_data, cut_rows, flag_rows):
    lon_count = lax.axis_size("lon")
    lon_index = lax.axis_index("lon")
    share = row_data.shape[0] // lon_count
    full_rows = lax.all_to_all(row_data, "lon", split_axis=0, concat_axis=1, tiled=True)
    my_cuts = lax.dynamic_slice_in_dim(cut_rows, lon_index * share, share)
    smoothed = project_rows(full_rows, my_cuts)
    returned = lax.all_to_all(smoothed, "lon", split_axis=1, concat_axis=0, tiled=True)
    return jnp.where(flag_rows[:, None] > 0, returned, row_data)


def polar_filter(row_data, cut_rows, flag_rows):
    return transpose_filter(row_data, cut_rows, flag_rows)


def on_device(adjoint, depth, zonal_coef, merid_coef, coriolis, layer_weight, cutoffs, polar_flags):
    fields, level_count, lat_rows, lon_cells = adjoint.shape
    lat_index = lax.axis_index("lat")
    lat_total = lat_rows * lax.axis_size("lat")
    stacked = adjoint.reshape(fields * level_count, lat_rows, lon_cells)
    bands = lax.all_to_all(stacked, "lat", split_axis=0, concat_axis=1, tiled=True)
    groups = bands.shape[0]
    polar_block = jnp.concatenate([bands[:, :POLE_ROWS], bands[:, lat_total - POLE_ROWS :]], axis=1)
    polar_cuts = jnp.concatenate([cutoffs[:POLE_ROWS], cutoffs[lat_total - POLE_ROWS :]])
    polar_marks = jnp.concatenate([polar_flags[:POLE_ROWS], polar_flags[lat_total - POLE_ROWS :]])
    row_data = polar_block.reshape(groups * 2 * POLE_ROWS, lon_cells)
    cut_rows = jnp.tile(polar_cuts, groups)
    flag_rows = jnp.tile(polar_marks, groups)
    treated = polar_filter(row_data, cut_rows, flag_rows)
    treated = treated.reshape(groups, 2 * POLE_ROWS, lon_cells)
    bands = jnp.concatenate(
        [
            treated[:, :POLE_ROWS],
            bands[:, POLE_ROWS : lat_total - POLE_ROWS],
            treated[:, POLE_ROWS:],
        ],
        axis=1,
    )
    filtered = lax.all_to_all(bands, "lat", split_axis=1, concat_axis=0, tiled=True).reshape(
        adjoint.shape
    )
    q_height = filtered[0]
    q_east = filtered[1]
    q_north = filtered[2]
    zonal_rows = lax.dynamic_slice_in_dim(zonal_coef, lat_index * lat_rows, lat_rows)[None, :, None]
    merid_rows = lax.dynamic_slice_in_dim(merid_coef, lat_index * lat_rows, lat_rows)[None, :, None]
    coriolis_rows = lax.dynamic_slice_in_dim(coriolis, lat_index * lat_rows, lat_rows)[
        None, :, None
    ]
    height_flux = depth.astype(jnp.float32) * q_height
    north_pair = jnp.stack([merid_rows * q_north, merid_rows * height_flux])
    north_rims = extended(north_pair, (("lat", 2),), 1, False)
    merid_diff = north_rims[:, :, :-2] - north_rims[:, :, 2:]
    east_pair = jnp.stack([q_east, height_flux])
    east_rims = extended(east_pair, (("lon", 3),), 1, True)
    zonal_diff = zonal_rows * (east_rims[..., :-2] - east_rims[..., 2:])
    column_force = -zonal_diff[0] - merid_diff[0]
    running = jnp.cumsum(column_force, axis=0)
    carried = entering(
        jnp.sum(column_force, axis=0), "lev", jnp.add, jnp.zeros((lat_rows, lon_cells), jnp.float32)
    )
    new_height = adjoint[0] + layer_weight[:, None, None] * (running + carried[None])
    new_east = adjoint[1] - zonal_diff[1] - coriolis_rows * q_north
    new_north = adjoint[2] - merid_diff[1] + coriolis_rows * q_east
    return jnp.stack([new_height, new_east, new_north])


RANK = 60
TILE = 256
LANES = 128


def halves(value):
    high = value.astype(jnp.bfloat16)
    return high, (value - high.astype(jnp.float32)).astype(jnp.bfloat16)


def split_table(value):
    high = np.asarray(value, np.float32).astype(ml_dtypes.bfloat16)
    low = (np.asarray(value, np.float32) - high.astype(np.float32)).astype(ml_dtypes.bfloat16)
    return high, low


@functools.lru_cache(maxsize=None)
def kernel_tables(cells):
    circle = 2 * cells

    def kernel(distance):
        wave = circle * np.sin(np.pi * (distance % (2 * circle)) / circle)
        return np.where(distance % circle == 0, 0.0, 1.0 / np.where(distance % circle == 0, 1.0, wave))

    n = np.arange(cells)
    rest = kernel(n[:, None] - n[None, :] - cells)
    columns, rows = [], []
    for _ in range(RANK):
        i, j = divmod(int(np.argmax(np.abs(rest))), cells)
        pivot = rest[i, j]
        size = np.sqrt(abs(pivot))
        u, v = rest[:, j] / pivot * size, rest[i, :] / size
        columns.append(u)
        rows.append(v)
        rest = rest - u[:, None] * v[None, :]
    project = np.stack(
        rows
        + [kernel(cells - 1 - n), kernel(0 - n), kernel(cells - 1 - n - cells), kernel(0 - n - cells)],
        axis=1,
    )
    expand = np.zeros((64, cells))
    expand[:RANK] = np.stack(columns)
    band = kernel(np.arange(2 * cells)[None, :] - np.arange(LANES)[:, None] - cells)
    return project, expand, band.astype(np.float32)


def project_kernel(x_ref, trig_ref, mix_ref, edge_ref, depth_ref, table_ref, out_ref):
    x = x_ref[...]
    fields, levels, rows, cells = x.shape
    cos, sin = trig_ref[0][None, None], trig_ref[1][None, None]

    def spectrum(value):
        high, low = halves(value.reshape(fields * levels * rows, cells))
        total = jnp.dot(high, table_ref[...], preferred_element_type=jnp.float32)
        total = total + jnp.dot(low, table_ref[...], preferred_element_type=jnp.float32)
        total = total + pltpu.roll(total, 64, 1)
        return total.reshape(fields, levels, rows, LANES)

    z = mix_ref[0][None, None] * spectrum(x * cos) + mix_ref[1][None, None] * spectrum(x * sin)
    lane = lax.broadcasted_iota(jnp.int32, (1, 1, rows, LANES), 3)
    z = z + jnp.where(lane == RANK, edge_ref[0][None, None] * x[..., cells - 1 :], 0.0)
    z = z + jnp.where(lane == RANK + 1, edge_ref[0][None, None] * x[..., :1], 0.0)
    depth = depth_ref[...].astype(jnp.float32)
    z = z + jnp.where(lane == 124, depth[None, :, :, cells - 1 :], 0.0)
    z = z + jnp.where(lane == 125, depth[None, :, :, :1], 0.0)
    out_ref[...] = z


def local_row(row, x_ref, trig_ref, coef_ref, band_ref, terms_ref, band_high, band_low, total_ref):
    cells = trig_ref.shape[2] // 2
    lines = cells // LANES * 8
    count = x_ref.shape[0] // lines
    blocks = cells // TILE
    chosen = lax.broadcasted_iota(jnp.int32, (8, LANES), 0) == row

    def line(values):
        return jnp.sum(jnp.where(chosen, values, 0.0), axis=0, keepdims=True)

    def strip(block):
        return pl.ds(block * 8 + row, count, stride=lines)

    coef = line(coef_ref[...])
    keep = coef[:, 3:4]
    for block in range(blocks):
        x = jnp.concatenate([x_ref[strip(2 * block), :], x_ref[strip(2 * block + 1), :]], axis=1)
        high, low = halves(x)
        at = pl.ds(block * count, count)
        terms_ref[at, :] = jnp.concatenate([high, low, high], axis=1)
        total_ref[at, :] = keep * x

    def upright(which):
        values = coef[:, 4:5] * line(trig_ref[which, :, cells : cells + LANES])
        return jnp.broadcast_to(values, (LANES, LANES)).T

    inner_cos, inner_sin = upright(0), upright(1)
    for block in range(2 * cells // LANES):
        at = pl.ds(block * LANES, LANES)
        value = band_ref[:, at] * (line(trig_ref[1, :, at]) * inner_cos - line(trig_ref[0, :, at]) * inner_sin)
        high, low = halves(value)
        band_high[:, at] = high
        band_low[:, at] = low
    for shift in range(1 - blocks, blocks):
        first = cells + TILE * shift
        weights = jnp.concatenate(
            [
                table[:, from_ : from_ + TILE]
                for table in (band_high, band_high, band_low)
                for from_ in (first, first - LANES)
            ],
            axis=0,
        )
        start, stop = max(0, -shift), min(blocks, blocks - shift)
        source = pl.ds(start * count, (stop - start) * count)
        target = pl.ds((start + shift) * count, (stop - start) * count)
        value = jnp.dot(terms_ref[source, :], weights, preferred_element_type=jnp.float32)
        total_ref[target, :] += value


def rim_kernel(x_ref, trig_ref, coef_ref, band_ref, y_ref, *scratch):
    local_row(pl.program_id(0) * 7, x_ref, trig_ref, coef_ref, band_ref, *scratch)
    total_ref = scratch[-1]
    count = y_ref.shape[1]
    for block in range(y_ref.shape[2] // TILE):
        y_ref[0, :, pl.ds(block * TILE, TILE)] = total_ref[pl.ds(block * count, count), :]


def inner_kernel(x_ref, trig_ref, coef_ref, band_ref, rim_ref, sent_ref, ends_ref, y_ref, *scratch):
    del sent_ref, ends_ref
    row = pl.program_id(0)
    _, count, cells = rim_ref.shape
    lines = cells // LANES * 8
    total_ref = scratch[-1]
    is_rim = jnp.logical_or(row == 0, row == 7)

    @pl.when(jnp.logical_not(is_rim))
    def _():
        local_row(row, x_ref, trig_ref, coef_ref, band_ref, *scratch)
        for block in range(cells // LANES):
            value = total_ref[pl.ds(block // 2 * count, count), pl.ds(block % 2 * LANES, LANES)]
            y_ref[pl.ds(block * 8 + row, count, stride=lines), :] = value

    @pl.when(is_rim)
    def _():
        for block in range(cells // LANES):
            value = rim_ref[row // 7, :, pl.ds(block * LANES, LANES)]
            y_ref[pl.ds(block * 8 + row, count, stride=lines), :] = value


def expanded(z, table_ref):
    turned = pltpu.roll(z, 64, 1)
    first = lax.broadcasted_iota(jnp.int32, z.shape, 1) < 64
    results = []
    for twice in (jnp.where(first, z, turned), jnp.where(first, turned, z)):
        terms = jnp.concatenate(halves(twice), axis=1)
        results.append(jnp.dot(terms, table_ref[...], preferred_element_type=jnp.float32))
    return results


def border_kernel(z_ref, y_ref, trig_ref, coef_ref, depth_ref, expand_ref, first_ref, last_ref):
    _, count, cells = y_ref.shape
    levels = depth_ref.shape[0]
    depth = depth_ref[...].astype(jnp.float32)
    for turn, row, ref in ((0, 0, first_ref), (1, 7, last_ref)):
        z = z_ref[pl.ds(row, count, stride=8), :]
        with_cos, with_sin = expanded(z, expand_ref)
        q = y_ref[turn] + trig_ref[0, row : row + 1] * with_cos + trig_ref[1, row : row + 1] * with_sin
        merid = coef_ref[row : row + 1, 1:2]
        ref[0] = merid * q[2 * levels :]
        ref[1] = merid * (depth[:, row, :] * q[:levels])


def final_kernel(
    weight_ref, x_ref, y_ref, z_ref, trig_ref, coef_ref, depth_ref, expand_ref, before_ref, after_ref, rims_ref,
    out_ref, q_ref, run_ref,
):
    step = pl.program_id(0)
    fields, levels, rows, cells = x_ref.shape
    coef = coef_ref[...]
    zonal, merid, coriolis = coef[:, 0:1], coef[:, 1:2], coef[:, 2:3]
    row = lax.broadcasted_iota(jnp.int32, (rows, cells), 0)
    column = lax.broadcasted_iota(jnp.int32, (rows, cells), 1)

    z = z_ref[...].reshape(fields * levels * rows, LANES)
    q = y_ref[...]
    for turn, value in enumerate(expanded(z, expand_ref)):
        q = q + trig_ref[turn][None, None] * value.reshape(fields, levels, rows, cells)
    q_ref[...] = q

    def zonal_adjoint(value, west, east):
        left = jnp.where(column == 0, west, pltpu.roll(value, 1, 1))
        right = jnp.where(column == cells - 1, east, pltpu.roll(value, cells - 1, 1))
        return zonal * (left - right)

    def merid_adjoint(value, before, after):
        value = merid * value
        up = jnp.where(row == 0, before, pltpu.roll(value, 1, 0))
        down = jnp.where(row == rows - 1, after, pltpu.roll(value, rows - 1, 0))
        return up - down

    @pl.when(step == 0)
    def _():
        run_ref[...] = jnp.zeros_like(run_ref)

    for level in range(levels):
        height, east, north = q_ref[0, level], q_ref[1, level], q_ref[2, level]
        flux = depth_ref[level].astype(jnp.float32) * height
        rims = rims_ref[level]
        line = pl.ds(level, 1)
        run_ref[...] -= zonal_adjoint(east, rims[:, 0:1], rims[:, 1:2]) + merid_adjoint(
            north, before_ref[0, line, :], after_ref[0, line, :]
        )
        out_ref[0, level] = x_ref[0, level] + weight_ref[step * levels + level] * run_ref[...]
        out_ref[1, level] = x_ref[1, level] - zonal_adjoint(flux, rims[:, 2:3], rims[:, 3:4]) - coriolis * north
        out_ref[2, level] = (
            x_ref[2, level]
            - merid_adjoint(flux, before_ref[1, line, :], after_ref[1, line, :])
            + coriolis * east
        )


def whole(array):
    shape = array.shape
    return pl.BlockSpec(shape, lambda *_: (0,) * len(shape))


def on_pair(adjoint, depth, zonal_coef, merid_coef, coriolis, layer_weight, cutoffs, polar_flags):
    fields, level_count, rows, cells = adjoint.shape
    circle = 2 * cells
    lat_count = lax.axis_size("lat")
    first_row = lax.axis_index("lat") * rows
    project, expand, band = kernel_tables(cells)
    project_high, project_low = split_table(project)
    project_table = jnp.asarray(np.concatenate([project_high, project_low], axis=1))
    expand_high, expand_low = split_table(expand)
    expand_table = jnp.asarray(
        np.concatenate([expand_high, expand_low, expand_high, np.zeros_like(expand_high)])
    )

    def mine(values):
        return lax.dynamic_slice_in_dim(values, first_row, rows)

    cuts, flags = mine(cutoffs), mine(polar_flags)
    kept = 2 * cuts + 1
    offsets = lax.iota(jnp.int32, circle) - cells
    phase = (kept[:, None] * offsets[None, :]) % (2 * circle)
    angle = phase.astype(jnp.float32) * (math.pi / circle)
    cos, sin = jnp.cos(angle), jnp.sin(angle)
    on = (flags > 0).astype(jnp.float32)[:, None]
    keep = jnp.where(flags > 0, kept.astype(jnp.float32) / circle, 1.0)[:, None]
    sign = on * jnp.where(cuts % 2 == 0, -1.0, 1.0)[:, None]
    own_cos, own_sin = cos[:, cells:], sin[:, cells:]
    trig = jnp.stack([own_cos, own_sin])
    cross = jnp.stack([sign * own_cos, sign * own_sin])
    around = jnp.stack([cos, sin])
    one, zero = jnp.ones((rows, RANK), jnp.float32), jnp.zeros((rows, RANK), jnp.float32)
    blank = jnp.zeros((rows, 4), jnp.float32)
    end_cos, end_sin = own_cos[:, cells - 1 :], own_sin[:, cells - 1 :]
    start_cos, start_sin = own_cos[:, :1], own_sin[:, :1]
    mix = jnp.stack(
        [
            jnp.concatenate(
                [one, on * end_sin, on * start_sin, sign * end_cos, sign * start_cos, zero, blank], axis=1
            ),
            jnp.concatenate(
                [zero, -on * end_cos, -on * start_cos, sign * end_sin, sign * start_sin, one, blank], axis=1
            ),
        ]
    )
    coef = jnp.concatenate(
        [
            mine(zonal_coef)[:, None],
            mine(merid_coef)[:, None],
            mine(coriolis)[:, None],
            keep,
            on,
            jnp.zeros((rows, LANES - 5), jnp.float32),
        ],
        axis=1,
    )
    edge = keep[None]

    part = 8
    steps = level_count // part
    four = pl.BlockSpec((fields, part, rows, cells), lambda i: (0, i, 0, 0))
    three = pl.BlockSpec((part, rows, cells), lambda i: (i, 0, 0))
    code = pl.BlockSpec((fields, part, rows, LANES), lambda i: (0, i, 0, 0))
    lines = pl.BlockSpec((2, part, cells), lambda i: (0, i, 0))
    limit = pltpu.CompilerParams(vmem_limit_bytes=48 * 2**20)
    count = fields * level_count * rows

    z = pl.pallas_call(
        project_kernel,
        grid=(steps,),
        in_specs=[four, whole(trig), whole(mix), whole(edge), three, whole(project_table)],
        out_specs=code,
        out_shape=jax.ShapeDtypeStruct((fields, level_count, rows, LANES), jnp.float32),
        compiler_params=limit,
    )(adjoint, trig, mix, edge, depth, project_table)
    arrived = lax.ppermute(z, "lon", [(0, 1), (1, 0)])

    circles = fields * level_count
    tiles = (circles, rows, cells // LANES, LANES)
    flat = adjoint.reshape(tiles).transpose(0, 2, 1, 3).reshape(-1, LANES)
    strip = circles * cells // TILE
    scratch = [
        pltpu.VMEM((strip, 3 * TILE), jnp.bfloat16),
        pltpu.VMEM((LANES, circle), jnp.bfloat16),
        pltpu.VMEM((LANES, circle), jnp.bfloat16),
        pltpu.VMEM((strip, TILE), jnp.float32),
    ]
    band = jnp.asarray(band)

    def cost(done):
        return pl.CostEstimate(
            flops=6 * done * circles * cells * cells, bytes_accessed=8 * count * cells, transcendentals=0
        )

    rim = pl.pallas_call(
        rim_kernel,
        grid=(2,),
        in_specs=[whole(flat), whole(around), whole(coef), whole(band)],
        out_specs=pl.BlockSpec((1, circles, cells), lambda i: (i, 0, 0)),
        out_shape=jax.ShapeDtypeStruct((2, circles, cells), jnp.float32),
        scratch_shapes=scratch,
        cost_estimate=cost(2),
        compiler_params=limit,
    )(flat, around, coef, band)

    sent = arrived.reshape(count, LANES)
    edges = jax.ShapeDtypeStruct((2, level_count, cells), jnp.float32)
    first, last = pl.pallas_call(
        border_kernel,
        grid=(1,),
        in_specs=[whole(sent), whole(rim), whole(cross), whole(coef), whole(depth), whole(expand_table)],
        out_specs=[whole(edges), whole(edges)],
        out_shape=[edges, edges],
        compiler_params=limit,
    )(sent, rim, cross, coef, depth, expand_table)
    before = lax.ppermute(last, "lat", [(i, i + 1) for i in range(lat_count - 1)])
    after = lax.ppermute(first, "lat", [(i + 1, i) for i in range(lat_count - 1)])

    rims = arrived[:2, ..., RANK : RANK + 2] + z[:2, ..., RANK + 2 : RANK + 4]
    rims = jnp.concatenate([rims[1], rims[0] * arrived[0, ..., 124:126]], axis=-1)

    y = pl.pallas_call(
        inner_kernel,
        grid=(rows,),
        in_specs=[
            whole(flat),
            whole(around),
            whole(coef),
            whole(band),
            whole(rim),
            pl.BlockSpec(memory_space=pl.ANY),
            pl.BlockSpec(memory_space=pl.ANY),
        ],
        out_specs=whole(flat),
        out_shape=jax.ShapeDtypeStruct(flat.shape, jnp.float32),
        scratch_shapes=scratch,
        cost_estimate=cost(rows - 2),
        compiler_params=limit,
    )(flat, around, coef, band, rim, first, rims)
    y = y.reshape(tiles[0], tiles[2], rows, LANES).transpose(0, 2, 1, 3).reshape(adjoint.shape)

    return pl.pallas_call(
        final_kernel,
        grid=(steps,),
        in_specs=[
            pl.BlockSpec(memory_space=pltpu.SMEM),
            four,
            four,
            code,
            whole(cross),
            whole(coef),
            three,
            whole(expand_table),
            lines,
            lines,
            pl.BlockSpec((part, rows, 4), lambda i: (i, 0, 0)),
        ],
        out_specs=four,
        out_shape=jax.ShapeDtypeStruct(adjoint.shape, jnp.float32),
        scratch_shapes=[
            pltpu.VMEM((fields, part, rows, cells), jnp.float32),
            pltpu.VMEM((rows, cells), jnp.float32),
        ],
        compiler_params=limit,
    )(layer_weight, adjoint, y, arrived, cross, coef, depth, expand_table, before, after, rims)


def plan_for(mesh):
    return on_pair if mesh.shape["lon"] == 2 and mesh.shape["lev"] == 1 else on_device


def solution(mesh):
    return jax.shard_map(
        plan_for(mesh),
        mesh=mesh,
        in_specs=(
            P("member", "lev", "lat", "lon"),
            P("lev", "lat", "lon"),
            P(),
            P(),
            P(),
            P("lev"),
            P(),
            P(),
        ),
        out_specs=P("member", "lev", "lat", "lon"),
        check_vma=False,
    )
```

```python
import functools
import math

import jax
import jax.numpy as jnp
import ml_dtypes
import numpy as np
from jax import lax
from jax.experimental import pallas as pl
from jax.experimental.pallas import tpu as pltpu
from jax.sharding import PartitionSpec as P

KMAX = 1024
POLE_ROWS = 24


def extended(cells, sides, width, closed):
    for axis, dim in sides:
        count = lax.axis_size(axis)
        ends = count if closed else count - 1
        head = lax.slice_in_dim(cells, 0, width, axis=dim)
        tail = lax.slice_in_dim(cells, cells.shape[dim] - width, cells.shape[dim], axis=dim)
        cells = jnp.concatenate(
            [
                lax.ppermute(tail, axis, [(i, (i + 1) % count) for i in range(ends)]),
                cells,
                lax.ppermute(head, axis, [((i + 1) % count, i) for i in range(ends)]),
            ],
            axis=dim,
        )
    return cells


def entering(value, axis, join, neutral):
    count, mine = (lax.axis_size(axis), lax.axis_index(axis))
    pieces = lax.all_gather(value, axis)
    total = jnp.full_like(value, 0) + jnp.asarray(neutral, value.dtype)

    def turn(position, total):
        longer = join(total, pieces[position])
        return jnp.where(position < mine, longer, total)

    return lax.fori_loop(0, count - 1, turn, total)


def wave_table(col_count, wave_start, wave_count, circle):
    columns = lax.iota(jnp.int32, col_count)
    wave_index = wave_start + lax.iota(jnp.int32, wave_count)
    phase = columns[:, None] * wave_index[None, :] % circle
    angle = phase.astype(jnp.float32) * (2.0 * math.pi / circle)
    return jnp.concatenate([jnp.cos(angle), jnp.sin(angle)], axis=1)


def keep_weights(cut_rows, wave_start, wave_count, circle):
    wave_index = wave_start + lax.iota(jnp.int32, wave_count)
    factor = jnp.where(wave_index == 0, 1.0, 2.0) / circle
    kept = (wave_index[None, :] <= cut_rows[:, None]).astype(jnp.float32) * factor[None, :]
    return jnp.concatenate([kept, kept], axis=1)


def block_width():
    return min(KMAX, 128)


def project_rows(row_data, cut_rows):
    circle = row_data.shape[1]
    width = block_width()
    result = jnp.zeros(row_data.shape, jnp.float32)
    for block_index in range(KMAX // width):
        table = wave_table(circle, block_index * width, width, circle)
        coefs = jnp.dot(
            row_data, table, precision=lax.Precision.HIGHEST, preferred_element_type=jnp.float32
        )
        weights = keep_weights(cut_rows, block_index * width, width, circle)
        result = result + jnp.dot(
            coefs * weights,
            table.T,
            precision=lax.Precision.HIGHEST,
            preferred_element_type=jnp.float32,
        )
    return result


def transpose_filter(row_data, cut_rows, flag_rows):
    lon_count = lax.axis_size("lon")
    lon_index = lax.axis_index("lon")
    share = row_data.shape[0] // lon_count
    full_rows = lax.all_to_all(row_data, "lon", split_axis=0, concat_axis=1, tiled=True)
    my_cuts = lax.dynamic_slice_in_dim(cut_rows, lon_index * share, share)
    smoothed = project_rows(full_rows, my_cuts)
    returned = lax.all_to_all(smoothed, "lon", split_axis=1, concat_axis=0, tiled=True)
    return jnp.where(flag_rows[:, None] > 0, returned, row_data)


def polar_filter(row_data, cut_rows, flag_rows):
    return transpose_filter(row_data, cut_rows, flag_rows)


def on_device(adjoint, depth, zonal_coef, merid_coef, coriolis, layer_weight, cutoffs, polar_flags):
    fields, level_count, lat_rows, lon_cells = adjoint.shape
    lat_index = lax.axis_index("lat")
    lat_total = lat_rows * lax.axis_size("lat")
    stacked = adjoint.reshape(fields * level_count, lat_rows, lon_cells)
    bands = lax.all_to_all(stacked, "lat", split_axis=0, concat_axis=1, tiled=True)
    groups = bands.shape[0]
    polar_block = jnp.concatenate([bands[:, :POLE_ROWS], bands[:, lat_total - POLE_ROWS :]], axis=1)
    polar_cuts = jnp.concatenate([cutoffs[:POLE_ROWS], cutoffs[lat_total - POLE_ROWS :]])
    polar_marks = jnp.concatenate([polar_flags[:POLE_ROWS], polar_flags[lat_total - POLE_ROWS :]])
    row_data = polar_block.reshape(groups * 2 * POLE_ROWS, lon_cells)
    cut_rows = jnp.tile(polar_cuts, groups)
    flag_rows = jnp.tile(polar_marks, groups)
    treated = polar_filter(row_data, cut_rows, flag_rows)
    treated = treated.reshape(groups, 2 * POLE_ROWS, lon_cells)
    bands = jnp.concatenate(
        [
            treated[:, :POLE_ROWS],
            bands[:, POLE_ROWS : lat_total - POLE_ROWS],
            treated[:, POLE_ROWS:],
        ],
        axis=1,
    )
    filtered = lax.all_to_all(bands, "lat", split_axis=1, concat_axis=0, tiled=True).reshape(
        adjoint.shape
    )
    q_height = filtered[0]
    q_east = filtered[1]
    q_north = filtered[2]
    zonal_rows = lax.dynamic_slice_in_dim(zonal_coef, lat_index * lat_rows, lat_rows)[None, :, None]
    merid_rows = lax.dynamic_slice_in_dim(merid_coef, lat_index * lat_rows, lat_rows)[None, :, None]
    coriolis_rows = lax.dynamic_slice_in_dim(coriolis, lat_index * lat_rows, lat_rows)[
        None, :, None
    ]
    height_flux = depth.astype(jnp.float32) * q_height
    north_pair = jnp.stack([merid_rows * q_north, merid_rows * height_flux])
    north_rims = extended(north_pair, (("lat", 2),), 1, False)
    merid_diff = north_rims[:, :, :-2] - north_rims[:, :, 2:]
    east_pair = jnp.stack([q_east, height_flux])
    east_rims = extended(east_pair, (("lon", 3),), 1, True)
    zonal_diff = zonal_rows * (east_rims[..., :-2] - east_rims[..., 2:])
    column_force = -zonal_diff[0] - merid_diff[0]
    running = jnp.cumsum(column_force, axis=0)
    carried = entering(
        jnp.sum(column_force, axis=0), "lev", jnp.add, jnp.zeros((lat_rows, lon_cells), jnp.float32)
    )
    new_height = adjoint[0] + layer_weight[:, None, None] * (running + carried[None])
    new_east = adjoint[1] - zonal_diff[1] - coriolis_rows * q_north
    new_north = adjoint[2] - merid_diff[1] + coriolis_rows * q_east
    return jnp.stack([new_height, new_east, new_north])


RANK = 60
TILE = 256
LANES = 128


def halves(value):
    high = value.astype(jnp.bfloat16)
    return high, (value - high.astype(jnp.float32)).astype(jnp.bfloat16)


def split_table(value):
    high = np.asarray(value, np.float32).astype(ml_dtypes.bfloat16)
    low = (np.asarray(value, np.float32) - high.astype(np.float32)).astype(ml_dtypes.bfloat16)
    return high, low


@functools.lru_cache(maxsize=None)
def kernel_tables(cells):
    circle = 2 * cells

    def kernel(distance):
        wave = circle * np.sin(np.pi * (distance % (2 * circle)) / circle)
        return np.where(distance % circle == 0, 0.0, 1.0 / np.where(distance % circle == 0, 1.0, wave))

    n = np.arange(cells)
    rest = kernel(n[:, None] - n[None, :] - cells)
    columns, rows = [], []
    for _ in range(RANK):
        i, j = divmod(int(np.argmax(np.abs(rest))), cells)
        pivot = rest[i, j]
        size = np.sqrt(abs(pivot))
        u, v = rest[:, j] / pivot * size, rest[i, :] / size
        columns.append(u)
        rows.append(v)
        rest = rest - u[:, None] * v[None, :]
    project = np.stack(
        rows
        + [kernel(cells - 1 - n), kernel(0 - n), kernel(cells - 1 - n - cells), kernel(0 - n - cells)],
        axis=1,
    )
    expand = np.zeros((64, cells))
    expand[:RANK] = np.stack(columns)
    band = kernel(np.arange(2 * cells)[None, :] - np.arange(LANES)[:, None] - cells)
    return project, expand, band.astype(np.float32)


def project_kernel(x_ref, trig_ref, mix_ref, edge_ref, depth_ref, table_ref, out_ref):
    x = x_ref[...]
    fields, levels, rows, cells = x.shape
    cos, sin = trig_ref[0][None, None], trig_ref[1][None, None]

    def spectrum(value):
        high, low = halves(value.reshape(fields * levels * rows, cells))
        total = jnp.dot(high, table_ref[...], preferred_element_type=jnp.float32)
        total = total + jnp.dot(low, table_ref[...], preferred_element_type=jnp.float32)
        total = total + pltpu.roll(total, 64, 1)
        return total.reshape(fields, levels, rows, LANES)

    z = mix_ref[0][None, None] * spectrum(x * cos) + mix_ref[1][None, None] * spectrum(x * sin)
    lane = lax.broadcasted_iota(jnp.int32, (1, 1, rows, LANES), 3)
    z = z + jnp.where(lane == RANK, edge_ref[0][None, None] * x[..., cells - 1 :], 0.0)
    z = z + jnp.where(lane == RANK + 1, edge_ref[0][None, None] * x[..., :1], 0.0)
    depth = depth_ref[...].astype(jnp.float32)
    z = z + jnp.where(lane == 124, depth[None, :, :, cells - 1 :], 0.0)
    z = z + jnp.where(lane == 125, depth[None, :, :, :1], 0.0)
    out_ref[...] = z


def local_row(row, x_ref, trig_ref, coef_ref, band_ref, terms_ref, band_high, band_low, total_ref):
    cells = trig_ref.shape[2] // 2
    lines = cells // LANES * 8
    count = x_ref.shape[0] // lines
    blocks = cells // TILE
    chosen = lax.broadcasted_iota(jnp.int32, (8, LANES), 0) == row

    def line(values):
        return jnp.sum(jnp.where(chosen, values, 0.0), axis=0, keepdims=True)

    def strip(block):
        return pl.ds(block * 8 + row, count, stride=lines)

    coef = line(coef_ref[...])
    keep = coef[:, 3:4]
    for block in range(blocks):
        x = jnp.concatenate([x_ref[strip(2 * block), :], x_ref[strip(2 * block + 1), :]], axis=1)
        high, low = halves(x)
        at = pl.ds(block * count, count)
        terms_ref[at, :] = jnp.concatenate([high, low, high], axis=1)
        total_ref[at, :] = keep * x

    def upright(which):
        values = coef[:, 4:5] * line(trig_ref[which, :, cells : cells + LANES])
        return jnp.broadcast_to(values, (LANES, LANES)).T

    inner_cos, inner_sin = upright(0), upright(1)
    def build(block):
        at = pl.ds(block * LANES, LANES)
        value = band_ref[:, at] * (line(trig_ref[1, :, at]) * inner_cos - line(trig_ref[0, :, at]) * inner_sin)
        high, low = halves(value)
        band_high[:, at] = high
        band_low[:, at] = low

    def multiply(shift):
        first = cells + TILE * shift
        weights = jnp.concatenate(
            [
                table[:, from_ : from_ + TILE]
                for table in (band_high, band_high, band_low)
                for from_ in (first, first - LANES)
            ],
            axis=0,
        )
        start, stop = max(0, -shift), min(blocks, blocks - shift)
        source = pl.ds(start * count, (stop - start) * count)
        target = pl.ds((start + shift) * count, (stop - start) * count)
        value = jnp.dot(terms_ref[source, :], weights, preferred_element_type=jnp.float32)
        total_ref[target, :] += value

    builds = [functools.partial(build, block) for block in range(2 * cells // LANES)]
    return builds, [functools.partial(multiply, shift) for shift in range(1 - blocks, blocks)]


def local_pair(rows, *refs):
    arrays, scratch = refs[:4], refs[4:]
    builds, products = local_row(rows[0], *arrays, *scratch[:4])
    for build in builds:
        build()
    later_builds, later_products = local_row(rows[1], *arrays, *scratch[4:])
    for turn, product in enumerate(products):
        product()
        for build in later_builds[turn :: len(products)]:
            build()
    for product in later_products:
        product()


def rim_kernel(x_ref, trig_ref, coef_ref, band_ref, y_ref, *scratch):
    local_pair((0, 7), x_ref, trig_ref, coef_ref, band_ref, *scratch)
    count = y_ref.shape[1]
    for turn in range(2):
        for block in range(y_ref.shape[2] // TILE):
            y_ref[turn, :, pl.ds(block * TILE, TILE)] = scratch[4 * turn + 3][pl.ds(block * count, count), :]


def inner_kernel(x_ref, trig_ref, coef_ref, band_ref, rim_ref, sent_ref, ends_ref, y_ref, *scratch):
    del sent_ref, ends_ref
    step = pl.program_id(0)
    _, count, cells = rim_ref.shape
    lines = cells // LANES * 8

    @pl.when(step < 3)
    def _():
        local_pair((2 * step + 1, 2 * step + 2), x_ref, trig_ref, coef_ref, band_ref, *scratch)
        for turn in range(2):
            for block in range(cells // LANES):
                part = pl.ds(block // 2 * count, count)
                value = scratch[4 * turn + 3][part, pl.ds(block % 2 * LANES, LANES)]
                y_ref[pl.ds(block * 8 + 2 * step + 1 + turn, count, stride=lines), :] = value

    @pl.when(step == 3)
    def _():
        for turn in range(2):
            for block in range(cells // LANES):
                value = rim_ref[turn, :, pl.ds(block * LANES, LANES)]
                y_ref[pl.ds(block * 8 + 7 * turn, count, stride=lines), :] = value


def expanded(z, table_ref):
    turned = pltpu.roll(z, 64, 1)
    first = lax.broadcasted_iota(jnp.int32, z.shape, 1) < 64
    results = []
    for twice in (jnp.where(first, z, turned), jnp.where(first, turned, z)):
        terms = jnp.concatenate(halves(twice), axis=1)
        results.append(jnp.dot(terms, table_ref[...], preferred_element_type=jnp.float32))
    return results


def border_kernel(z_ref, y_ref, trig_ref, coef_ref, depth_ref, expand_ref, first_ref, last_ref):
    _, count, cells = y_ref.shape
    levels = depth_ref.shape[0]
    depth = depth_ref[...].astype(jnp.float32)
    for turn, row, ref in ((0, 0, first_ref), (1, 7, last_ref)):
        z = z_ref[pl.ds(row, count, stride=8), :]
        with_cos, with_sin = expanded(z, expand_ref)
        q = y_ref[turn] + trig_ref[0, row : row + 1] * with_cos + trig_ref[1, row : row + 1] * with_sin
        merid = coef_ref[row : row + 1, 1:2]
        ref[0] = merid * q[2 * levels :]
        ref[1] = merid * (depth[:, row, :] * q[:levels])


def final_kernel(
    weight_ref, x_ref, y_ref, z_ref, trig_ref, coef_ref, depth_ref, expand_ref, before_ref, after_ref, rims_ref,
    out_ref, q_ref, run_ref,
):
    step = pl.program_id(0)
    fields, levels, rows, cells = x_ref.shape
    coef = coef_ref[...]
    zonal, merid, coriolis = coef[:, 0:1], coef[:, 1:2], coef[:, 2:3]
    row = lax.broadcasted_iota(jnp.int32, (rows, cells), 0)
    column = lax.broadcasted_iota(jnp.int32, (rows, cells), 1)

    z = z_ref[...].reshape(fields * levels * rows, LANES)
    q = y_ref[...]
    for turn, value in enumerate(expanded(z, expand_ref)):
        q = q + trig_ref[turn][None, None] * value.reshape(fields, levels, rows, cells)
    q_ref[...] = q

    def zonal_adjoint(value, west, east):
        left = jnp.where(column == 0, west, pltpu.roll(value, 1, 1))
        right = jnp.where(column == cells - 1, east, pltpu.roll(value, cells - 1, 1))
        return zonal * (left - right)

    def merid_adjoint(value, before, after):
        value = merid * value
        up = jnp.where(row == 0, before, pltpu.roll(value, 1, 0))
        down = jnp.where(row == rows - 1, after, pltpu.roll(value, rows - 1, 0))
        return up - down

    @pl.when(step == 0)
    def _():
        run_ref[...] = jnp.zeros_like(run_ref)

    for level in range(levels):
        height, east, north = q_ref[0, level], q_ref[1, level], q_ref[2, level]
        flux = depth_ref[level].astype(jnp.float32) * height
        rims = rims_ref[level]
        line = pl.ds(level, 1)
        run_ref[...] -= zonal_adjoint(east, rims[:, 0:1], rims[:, 1:2]) + merid_adjoint(
            north, before_ref[0, line, :], after_ref[0, line, :]
        )
        out_ref[0, level] = x_ref[0, level] + weight_ref[step * levels + level] * run_ref[...]
        out_ref[1, level] = x_ref[1, level] - zonal_adjoint(flux, rims[:, 2:3], rims[:, 3:4]) - coriolis * north
        out_ref[2, level] = (
            x_ref[2, level]
            - merid_adjoint(flux, before_ref[1, line, :], after_ref[1, line, :])
            + coriolis * east
        )


def whole(array):
    shape = array.shape
    return pl.BlockSpec(shape, lambda *_: (0,) * len(shape))


def on_pair(adjoint, depth, zonal_coef, merid_coef, coriolis, layer_weight, cutoffs, polar_flags):
    fields, level_count, rows, cells = adjoint.shape
    circle = 2 * cells
    lat_count = lax.axis_size("lat")
    first_row = lax.axis_index("lat") * rows
    project, expand, band = kernel_tables(cells)
    project_high, project_low = split_table(project)
    project_table = jnp.asarray(np.concatenate([project_high, project_low], axis=1))
    expand_high, expand_low = split_table(expand)
    expand_table = jnp.asarray(
        np.concatenate([expand_high, expand_low, expand_high, np.zeros_like(expand_high)])
    )

    def mine(values):
        return lax.dynamic_slice_in_dim(values, first_row, rows)

    cuts, flags = mine(cutoffs), mine(polar_flags)
    kept = 2 * cuts + 1
    offsets = lax.iota(jnp.int32, circle) - cells
    phase = (kept[:, None] * offsets[None, :]) % (2 * circle)
    angle = phase.astype(jnp.float32) * (math.pi / circle)
    cos, sin = jnp.cos(angle), jnp.sin(angle)
    on = (flags > 0).astype(jnp.float32)[:, None]
    keep = jnp.where(flags > 0, kept.astype(jnp.float32) / circle, 1.0)[:, None]
    sign = on * jnp.where(cuts % 2 == 0, -1.0, 1.0)[:, None]
    own_cos, own_sin = cos[:, cells:], sin[:, cells:]
    trig = jnp.stack([own_cos, own_sin])
    cross = jnp.stack([sign * own_cos, sign * own_sin])
    around = jnp.stack([cos, sin])
    one, zero = jnp.ones((rows, RANK), jnp.float32), jnp.zeros((rows, RANK), jnp.float32)
    blank = jnp.zeros((rows, 4), jnp.float32)
    end_cos, end_sin = own_cos[:, cells - 1 :], own_sin[:, cells - 1 :]
    start_cos, start_sin = own_cos[:, :1], own_sin[:, :1]
    mix = jnp.stack(
        [
            jnp.concatenate(
                [one, on * end_sin, on * start_sin, sign * end_cos, sign * start_cos, zero, blank], axis=1
            ),
            jnp.concatenate(
                [zero, -on * end_cos, -on * start_cos, sign * end_sin, sign * start_sin, one, blank], axis=1
            ),
        ]
    )
    coef = jnp.concatenate(
        [
            mine(zonal_coef)[:, None],
            mine(merid_coef)[:, None],
            mine(coriolis)[:, None],
            keep,
            on,
            jnp.zeros((rows, LANES - 5), jnp.float32),
        ],
        axis=1,
    )
    edge = keep[None]

    part = 8
    steps = level_count // part
    four = pl.BlockSpec((fields, part, rows, cells), lambda i: (0, i, 0, 0))
    three = pl.BlockSpec((part, rows, cells), lambda i: (i, 0, 0))
    code = pl.BlockSpec((fields, part, rows, LANES), lambda i: (0, i, 0, 0))
    lines = pl.BlockSpec((2, part, cells), lambda i: (0, i, 0))
    limit = pltpu.CompilerParams(vmem_limit_bytes=48 * 2**20)
    count = fields * level_count * rows

    z = pl.pallas_call(
        project_kernel,
        grid=(steps,),
        in_specs=[four, whole(trig), whole(mix), whole(edge), three, whole(project_table)],
        out_specs=code,
        out_shape=jax.ShapeDtypeStruct((fields, level_count, rows, LANES), jnp.float32),
        compiler_params=limit,
    )(adjoint, trig, mix, edge, depth, project_table)
    arrived = lax.ppermute(z, "lon", [(0, 1), (1, 0)])

    circles = fields * level_count
    tiles = (circles, rows, cells // LANES, LANES)
    flat = adjoint.reshape(tiles).transpose(0, 2, 1, 3).reshape(-1, LANES)
    strip = circles * cells // TILE
    scratch = [
        pltpu.VMEM((strip, 3 * TILE), jnp.bfloat16),
        pltpu.VMEM((LANES, circle), jnp.bfloat16),
        pltpu.VMEM((LANES, circle), jnp.bfloat16),
        pltpu.VMEM((strip, TILE), jnp.float32),
    ]
    band = jnp.asarray(band)

    def cost(done):
        return pl.CostEstimate(
            flops=6 * done * circles * cells * cells, bytes_accessed=8 * count * cells, transcendentals=0
        )

    rim = pl.pallas_call(
        rim_kernel,
        grid=(1,),
        in_specs=[whole(flat), whole(around), whole(coef), whole(band)],
        out_specs=pl.BlockSpec((2, circles, cells), lambda i: (0, 0, 0)),
        out_shape=jax.ShapeDtypeStruct((2, circles, cells), jnp.float32),
        scratch_shapes=2 * scratch,
        cost_estimate=cost(2),
        compiler_params=limit,
    )(flat, around, coef, band)

    sent = arrived.reshape(count, LANES)
    edges = jax.ShapeDtypeStruct((2, level_count, cells), jnp.float32)
    first, last = pl.pallas_call(
        border_kernel,
        grid=(1,),
        in_specs=[whole(sent), whole(rim), whole(cross), whole(coef), whole(depth), whole(expand_table)],
        out_specs=[whole(edges), whole(edges)],
        out_shape=[edges, edges],
        compiler_params=limit,
    )(sent, rim, cross, coef, depth, expand_table)
    before = lax.ppermute(last, "lat", [(i, i + 1) for i in range(lat_count - 1)])
    after = lax.ppermute(first, "lat", [(i + 1, i) for i in range(lat_count - 1)])

    rims = arrived[:2, ..., RANK : RANK + 2] + z[:2, ..., RANK + 2 : RANK + 4]
    rims = jnp.concatenate([rims[1], rims[0] * arrived[0, ..., 124:126]], axis=-1)

    y = pl.pallas_call(
        inner_kernel,
        grid=(rows // 2,),
        in_specs=[
            whole(flat),
            whole(around),
            whole(coef),
            whole(band),
            whole(rim),
            pl.BlockSpec(memory_space=pl.ANY),
            pl.BlockSpec(memory_space=pl.ANY),
        ],
        out_specs=whole(flat),
        out_shape=jax.ShapeDtypeStruct(flat.shape, jnp.float32),
        scratch_shapes=2 * scratch,
        cost_estimate=cost(rows - 2),
        compiler_params=limit,
    )(flat, around, coef, band, rim, first, rims)
    y = y.reshape(tiles[0], tiles[2], rows, LANES).transpose(0, 2, 1, 3).reshape(adjoint.shape)

    return pl.pallas_call(
        final_kernel,
        grid=(steps,),
        in_specs=[
            pl.BlockSpec(memory_space=pltpu.SMEM),
            four,
            four,
            code,
            whole(cross),
            whole(coef),
            three,
            whole(expand_table),
            lines,
            lines,
            pl.BlockSpec((part, rows, 4), lambda i: (i, 0, 0)),
        ],
        out_specs=four,
        out_shape=jax.ShapeDtypeStruct(adjoint.shape, jnp.float32),
        scratch_shapes=[
            pltpu.VMEM((fields, part, rows, cells), jnp.float32),
            pltpu.VMEM((rows, cells), jnp.float32),
        ],
        compiler_params=limit,
    )(layer_weight, adjoint, y, arrived, cross, coef, depth, expand_table, before, after, rims)


def plan_for(mesh):
    return on_pair if mesh.shape["lon"] == 2 and mesh.shape["lev"] == 1 else on_device


def solution(mesh):
    return jax.shard_map(
        plan_for(mesh),
        mesh=mesh,
        in_specs=(
            P("member", "lev", "lat", "lon"),
            P("lev", "lat", "lon"),
            P(),
            P(),
            P(),
            P("lev"),
            P(),
            P(),
        ),
        out_specs=P("member", "lev", "lat", "lon"),
        check_vma=False,
    )
```
